32 devices in a mesh: groups: 1, seq: 32 (over z, y, x, core).
Axes of the slice: x: 2, y: 2, z: 4, core: 2. Of those that a mesh axis runs over, the one named last changes fastest.
Arguments:
- query: bfloat16 [4096, 4096], P(('groups', 'seq')), may hold values from -20 to 20
- key: bfloat16 [4096, 512], P(('groups', 'seq')), may hold values from -20 to 20
- value: bfloat16 [4096, 512], P(('groups', 'seq')), may hold values from -6 to 6
- segment_ids: int32 [4096], P(('groups', 'seq')), may hold values from 0 to 15, never falling along the last dimension, each value on 1 to 384 neighbouring positions
- student_rows: bfloat16 [4096, 1536], P(('groups', 'seq')), may hold values from -6 to 6
- projection: bfloat16 [1536, 4096], P('seq'), may hold values from -0.15625 to 0.15625
- send_order: int32 [32, 128], P(('groups', 'seq')), may hold values from 0 to 127, each once within a row
Outputs:
- grad_rows: bfloat16 [4096, 1536], P(('groups', 'seq'))
- grad_proj: float32 [1536, 4096], P(('groups', 'seq'))
The draws below stay inside these ranges and needn't reach their ends.
Inputs may be any that keep to these rules, and one draw needn't show every extreme that they name: `segment_ids`: ids never fall along the sequence and every id is used; no document is longer than 384 tokens and one has exactly 384. `send_order`: each row is a permutation of the numbers below 128.
All inputs are finite; a program needn't handle non-finite values.
Results may differ from the reference program's by a relative error of at most 0.0045.
Values may be sent and summed in bfloat16 or wider, within the bound.
A program may use at most 192 MiB of HBM per device.

```python
import math
import jax
import jax.numpy as jnp
import numpy as np
from jax import lax

HQ = 32
KVH = 4
HD = 128
DS = 1536
REACH = 3
TOK_DEV = 128
TOKENS = 4096
MAXDOC = 384
N_SEQ = 32


def drawn_base(key):
    return jnp.clip(jax.random.normal(key, (TOKENS, KVH, HD), jnp.float32), -4.0, 4.0)


def draw_key(key, part):
    base = drawn_base(key)
    return base.reshape(TOKENS, KVH * HD).astype(jnp.bfloat16)


def draw_query(key, part):
    key = jax.random.fold_in(key, 7)
    fresh = jnp.clip(jax.random.normal(key, (TOKENS, KVH, HQ // KVH, HD), jnp.float32), -4.0, 4.0)
    return fresh.reshape(TOKENS, HQ * HD).astype(jnp.bfloat16)


def strengthened(result, stream_key, source, target, parts, factor):
    owner, partner = [(jnp.arange(result.shape[dim]) // (result.shape[dim] // parts)).reshape([-1 if axis == dim else 1 for axis in range(result.ndim)]) for dim in (source, target)]
    chosen = jax.random.permutation(stream_key, parts)[partner]
    strong = (owner == chosen) | (owner == (partner + parts // 2) % parts)
    return jnp.where(strong, factor * result, result)


def level_of(own_key, shape, split, least, top_value):
    factor_of = 1.0
    for dim, blocks in split:
        steps = jax.random.uniform(jax.random.fold_in(jax.random.fold_in(own_key, 6), dim), (blocks,), jnp.float32, least / len(split), top_value / len(split))
        factor_of = factor_of * jnp.repeat(jnp.exp(steps), shape[dim] // blocks).reshape((-1,) + (1,) * (len(shape) - 1 - dim))
    return factor_of


def profile(number_of, total, limit, slope):
    weights = [(1 << 20) // math.isqrt(grade ** slope) + 1 for grade in range(2, number_of + 1)]
    spare, given = total - limit - (number_of - 1), [1] * (number_of - 1)
    while spare > 0:
        candidates = [i for i in range(number_of - 1) if given[i] < limit]
        whole, left = sum([weights[i] for i in candidates]), spare
        for i in candidates:
            extra = min(limit - given[i], max(1, left * weights[i] // whole), spare)
            given[i] = given[i] + extra
            spare = spare - extra
    return np.array([limit] + given)


def ragged_sizes(key, amount, total, most, skew):
    if amount == 2:
        one = jax.random.randint(key, (), max(1, total - most), min(most, total - 1) + 1)
        return jnp.stack([one, total - one])
    sizes = jnp.asarray(profile(amount, total, most, skew), jnp.int32)
    twos = (amount - 1) // 2
    source_of, receiver = sizes[1:1 + 2 * twos:2], sizes[2:2 + 2 * twos:2]
    room = jnp.minimum(source_of - 1, most - receiver)
    passed = jax.random.randint(jax.random.fold_in(key, 1), (twos,), 0, 1 << 20) % (room + 1)
    sizes = sizes.at[1:1 + 2 * twos:2].set(source_of - passed).at[2:2 + 2 * twos:2].set(receiver + passed)
    return sizes[jax.random.permutation(jax.random.fold_in(key, 2), amount)]


def scatter_about(own_key, extent, deviation, reach, split=(), held_as=jnp.bfloat16):
    values = jax.random.normal(own_key, extent, jnp.float32) * deviation
    if len(split) > 0:
        values = level_of(own_key, extent, split, -0.22, 0.18) * values
    return jnp.clip(values, min=-reach, max=reach).astype(held_as)


def gaussian_with(stream_key, dims, deviation, bound, pieces, heavy, kind=jnp.bfloat16):
    array = deviation * jax.random.normal(stream_key, dims, jnp.float32)
    if pieces:
        array = array * level_of(stream_key, dims, pieces, -0.22, 0.18)
    return jnp.clip(strengthened(array, jax.random.fold_in(stream_key, 3), *heavy), -bound, bound).astype(kind)


def setup_inputs(seed: int = 0, part: int = 0) -> dict:
    seeds = jax.random.split(jax.random.key(seed), 8)
    own_keys = jax.random.split(jax.random.fold_in(seeds[7], part), 8)
    return {
        "query": draw_query(jax.random.fold_in(jax.random.fold_in(seeds[7], part), 71), part),
        "key": draw_key(jax.random.fold_in(jax.random.fold_in(seeds[7], part), 71), part),
        "value": scatter_about(own_keys[2], (TOKENS, KVH * HD), 1.0, 6.0, ((0, 32),)),
        "segment_ids": jnp.searchsorted(jnp.cumsum(ragged_sizes(own_keys[3], TOKENS // 256, TOKENS, MAXDOC, 2)), jnp.arange(TOKENS), side="right").astype(jnp.int32),
        "student_rows": gaussian_with(own_keys[4], (TOKENS, DS), 1.0, 6.0, ((0, 32),), (0, 1, 32, 2.75)),
        "projection": scatter_about(seeds[5], (DS, HQ * HD), DS ** -0.5, 0.15625, ((0, 32),)),
        "send_order": jax.vmap(lambda own: jax.random.permutation(own, TOK_DEV))(jax.random.split(own_keys[6], N_SEQ)).reshape((N_SEQ, TOK_DEV)).astype(jnp.int32),
    }


def reference(query, key, value, segment_ids, student_rows, projection, send_order):
    group_size = HQ // KVH
    places = jnp.arange(TOKENS, dtype=jnp.int32)
    doc_start = jnp.searchsorted(segment_ids, segment_ids, side="left").astype(jnp.int32)
    span = (REACH + 1) * TOK_DEV
    margin = REACH * TOK_DEV
    key_pad = jnp.concatenate([jnp.zeros((margin, KVH * HD), key.dtype), key], 0)
    value_pad = jnp.concatenate([jnp.zeros((margin, KVH * HD), value.dtype), value], 0)
    key_places = jnp.arange(TOKENS + margin, dtype=jnp.int32) - margin

    def attend(block):
        begin = (block * TOK_DEV).astype(jnp.int32)
        query_rows = lax.dynamic_slice_in_dim(query, begin, TOK_DEV, 0).reshape(TOK_DEV, KVH, group_size, HD).astype(jnp.float32)
        key_rows = lax.dynamic_slice_in_dim(key_pad, begin, span, 0).reshape(span, KVH, HD).astype(jnp.float32)
        value_rows = lax.dynamic_slice_in_dim(value_pad, begin, span, 0).reshape(span, KVH, HD).astype(jnp.float32)
        key_pos = lax.dynamic_slice_in_dim(key_places, begin, span, 0)
        query_pos = lax.dynamic_slice_in_dim(places, begin, TOK_DEV, 0)
        starts = lax.dynamic_slice_in_dim(doc_start, begin, TOK_DEV, 0)
        allowed = (key_pos[None, :] <= query_pos[:, None]) & (key_pos[None, :] >= starts[:, None])
        scores = jnp.einsum("qgjd,kgd->gjqk", query_rows, key_rows) * (HD ** -0.5)
        scores = jnp.where(allowed[None, None], scores, -jnp.inf)
        row_max = jnp.max(scores, axis=3, keepdims=True)
        weights = jnp.exp(scores - row_max)
        weights = (weights / jnp.sum(weights, axis=3, keepdims=True)).astype(jnp.bfloat16)
        context = jnp.einsum("gjqk,kgd->qgjd", weights.astype(jnp.float32), value_rows)
        return context.astype(jnp.bfloat16).reshape(TOK_DEV, HQ * HD)

    teacher = lax.map(attend, jnp.arange(N_SEQ, dtype=jnp.int32)).reshape(TOKENS, HQ * HD)
    rows_each = TOK_DEV // N_SEQ
    order = send_order.reshape(N_SEQ, N_SEQ, rows_each)
    source_base = (jnp.arange(N_SEQ, dtype=jnp.int32) * TOK_DEV)[:, None, None]
    picks = jnp.transpose(order + source_base, (1, 0, 2)).reshape(TOKENS).astype(jnp.int32)
    target = jnp.take(teacher, picks, axis=0)
    grad_scale = TOKENS ** -0.5

    def owner_step(total, owner):
        begin = (owner * TOK_DEV).astype(jnp.int32)
        rows_here = lax.dynamic_slice_in_dim(student_rows, begin, TOK_DEV, 0)
        target_here = lax.dynamic_slice_in_dim(target, begin, TOK_DEV, 0)
        predicted = jnp.dot(rows_here, projection, preferred_element_type=jnp.float32)
        residual = (predicted - target_here.astype(jnp.float32)).astype(jnp.bfloat16)
        grad_here = lax.dot_general(residual, projection, (((1,), (1,)), ((), ())), preferred_element_type=jnp.float32).astype(jnp.bfloat16)
        partial_term = lax.dot_general(rows_here, residual, (((0,), (0,)), ((), ())), preferred_element_type=jnp.float32) * grad_scale
        total = total + partial_term
        return total, grad_here

    start_total = jnp.zeros((DS, HQ * HD), jnp.float32)
    grad_proj, grad_blocks = lax.scan(owner_step, start_total, jnp.arange(N_SEQ, dtype=jnp.int32))
    grad_rows = grad_blocks.reshape(TOKENS, DS)
    return grad_rows, grad_proj
```

```python
import jax
import jax.numpy as jnp
from jax import lax
from jax.sharding import PartitionSpec as P

HQ = 32
KVH = 4
HD = 128
REACH = 3
COLS = 8


def shifted(value, axis, steps):
    count = lax.axis_size(axis)
    return lax.ppermute(value, axis, [(s, s + steps) for s in range(count - steps)])


def attention(query, key, value, segment_ids):
    rows = query.shape[0]
    per_group = HQ // KVH
    me = lax.axis_index("seq")
    ids = jnp.broadcast_to(segment_ids.astype(jnp.bfloat16)[:, None], (rows, HD))
    block = jnp.concatenate([key, value, ids], axis=1)
    blocks = [block] + [shifted(block, "seq", step) for step in range(1, REACH + 1)]
    flat = jnp.concatenate(blocks[::-1], axis=0)
    span = flat.shape[0]
    key_ids = flat[:, 2 * KVH * HD].astype(jnp.int32)
    places = jnp.arange(rows, dtype=jnp.int32) + REACH * rows
    key_places = jnp.arange(span, dtype=jnp.int32)
    allowed = (
        (key_places[None, :] <= places[:, None])
        & (key_ids[None, :] == segment_ids[:, None])
        & (key_places[None, :] >= (REACH - me) * rows)
    )
    scale = HD ** (-0.5)
    outputs = []
    for g in range(KVH):
        q = query[:, g * per_group * HD : (g + 1) * per_group * HD].reshape(rows, per_group, HD)
        k = flat[:, g * HD : (g + 1) * HD]
        v = flat[:, (KVH + g) * HD : (KVH + g + 1) * HD]
        scores = jnp.einsum("qhd,kd->hqk", q, k, preferred_element_type=jnp.float32) * scale
        scores = jnp.where(allowed[None], scores, -jnp.inf)
        top = jnp.max(scores, axis=2, keepdims=True)
        weights = jnp.exp(scores - top)
        weights = (weights / jnp.sum(weights, axis=2, keepdims=True)).astype(jnp.bfloat16)
        context = jnp.einsum("hqk,kd->qhd", weights, v, preferred_element_type=jnp.float32)
        outputs.append(context.astype(jnp.bfloat16).reshape(rows, per_group * HD))
    return jnp.concatenate(outputs, axis=1)


def local(query, key, value, segment_ids, student_rows, projection, send_order):
    rows = query.shape[0]
    n = lax.axis_size("seq")
    cols = COLS
    bands = n // cols
    width = HQ * HD // cols
    depth = projection.shape[0]
    ds = student_rows.shape[1]
    share = rows // n
    near = [[b * cols + c for c in range(cols)] for b in range(bands)]
    far = [[b * cols + c for b in range(bands)] for c in range(cols)]

    band_rows = lax.all_gather(student_rows, "seq", axis=0, tiled=True, axis_index_groups=near)
    pieces = projection.reshape(depth, cols, width).transpose(1, 0, 2)
    pieces = lax.all_to_all(
        pieces, "seq", split_axis=0, concat_axis=0, tiled=True, axis_index_groups=near
    )
    column = lax.all_gather(
        pieces.reshape(cols * depth, width), "seq", axis=0, tiled=True, axis_index_groups=far
    )
    teacher = attention(query, key, value, segment_ids)
    outgoing = jnp.take(teacher, send_order[0], axis=0)
    outgoing = outgoing.reshape(bands, cols * share, cols, width).transpose(0, 2, 1, 3)
    arrived = lax.all_to_all(
        outgoing.reshape(n, cols * share, width), "seq", split_axis=0, concat_axis=0, tiled=True
    )
    target = arrived.reshape(n, cols, share, width).transpose(1, 0, 2, 3).reshape(cols * rows, width)
    predicted = jnp.dot(band_rows, column, preferred_element_type=jnp.float32)
    residual = (predicted - target.astype(jnp.float32)).astype(jnp.bfloat16)
    proj_part = lax.dot_general(
        band_rows, residual, (((0,), (0,)), ((), ())), preferred_element_type=jnp.float32
    ).astype(jnp.bfloat16)
    proj_parts = lax.all_to_all(
        proj_part.reshape(n, depth, width), "seq", split_axis=0, concat_axis=0, tiled=True
    )
    rows_part = lax.dot_general(
        residual, column, (((1,), (1,)), ((), ())), preferred_element_type=jnp.float32
    ).astype(jnp.bfloat16)
    rows_parts = lax.all_to_all(
        rows_part.reshape(cols, rows, ds),
        "seq", split_axis=0, concat_axis=0, tiled=True, axis_index_groups=near,
    )
    grad_rows = jnp.sum(rows_parts.astype(jnp.float32), axis=0).astype(jnp.bfloat16)
    grad_scale = (rows * n) ** (-0.5)
    summed = jnp.sum(proj_parts.reshape(bands, cols, depth, width).astype(jnp.float32), axis=0)
    grad_proj = (summed * grad_scale).transpose(1, 0, 2).reshape(depth, cols * width)
    return (grad_rows, grad_proj)


def solution(mesh):
    both = ("groups", "seq")
    return jax.shard_map(
        local,
        mesh=mesh,
        in_specs=(
            P(both, None), P(both, None), P(both, None), P(both), P(both, None),
            P("seq", None), P(both, None),
        ),
        out_specs=(P(both, None), P(both, None)),
        check_vma=False,
    )
```

```python
import functools

import jax
import jax.numpy as jnp
from jax import lax
from jax.experimental import pallas as pl
from jax.experimental.pallas import tpu as pltpu
from jax.sharding import PartitionSpec as P

HQ = 32
KVH = 4
HD = 128
REACH = 3
COLS = 8
MESH = pl.DeviceIdType.MESH


def reach_kernel(n, seg_ref, segcol_ref, order_ref, query_ref, pairs_ref, rows_ref, proj_ref,
                 band_ref, column_ref, arrived_ref, pairs_in, ids_in, outgoing,
                 pair_send, pair_recv, id_send, id_recv, col_send, col_recv,
                 row_send, row_recv, out_send, out_recv, own_sem):
    me = lax.axis_index("seq")
    cols = COLS
    bands = n // cols
    my_band, my_col = me // cols, me % cols
    rows = query_ref.shape[0]
    width = HQ * HD // cols
    heads = HQ // cols

    def remote(src, dst, send, recv, peer):
        return pltpu.make_async_remote_copy(
            src_ref=src, dst_ref=dst, send_sem=send, recv_sem=recv,
            device_id={"seq": peer}, device_id_type=MESH)

    def pair_copy(k):
        return remote(pairs_ref, pairs_in.at[k - 1], pair_send.at[k - 1], pair_recv.at[k - 1], (me + k) % n)

    def id_copy(k):
        return remote(seg_ref, ids_in.at[k - 1], id_send.at[k - 1], id_recv.at[k - 1], (me + k) % n)

    def col_copy(peer, slot, place):
        block = proj_ref.at[:, pl.ds(pl.multiple_of((peer % cols) * width, width), width)]
        return remote(block, column_ref.at[place], col_send.at[slot], col_recv.at[place], peer)

    def row_copy(peer, slot, place):
        return remote(rows_ref, band_ref.at[place], row_send.at[slot], row_recv.at[place], peer)

    def out_copy(peer, place):
        return remote(outgoing.at[peer % cols, peer // cols], arrived_ref.at[place],
                      out_send.at[peer], out_recv.at[place], peer)

    own = [
        pltpu.make_async_copy(rows_ref, band_ref.at[my_col], own_sem.at[0]),
        pltpu.make_async_copy(
            proj_ref.at[:, pl.ds(pl.multiple_of(my_col * width, width), width)],
            column_ref.at[me], own_sem.at[1]),
        pltpu.make_async_copy(outgoing.at[my_col, my_band], arrived_ref.at[me], own_sem.at[2]),
    ]

    barrier = pltpu.get_barrier_semaphore()

    @pl.loop(1, n)
    def _(k):
        pl.semaphore_signal(barrier, inc=1, device_id={"seq": (me + k) % n}, device_id_type=MESH)

    pl.semaphore_wait(barrier, n - 1)
    for k in range(1, REACH + 1):
        id_copy(k).start()
        pair_copy(k).start()
    own[0].start()
    own[1].start()

    @pl.loop(1, cols)
    def _(k):
        row_copy(my_band * cols + (my_col + k) % cols, k, my_col).start()

    @pl.loop(1, n)
    def _(k):
        col_copy((me + k) % n, k, me).start()

    for k in range(1, REACH + 1):
        id_copy(k).wait()
        pair_copy(k).wait()

    key_ids = jnp.concatenate([seg_ref[0:1, :]] + [ids_in[k, 0:1, :] for k in range(REACH)], axis=1)
    span = (REACH + 1) * rows
    place = lax.broadcasted_iota(jnp.int32, (rows, span), 1)
    back = place // rows
    at = place - 2 * rows * back
    row = lax.broadcasted_iota(jnp.int32, (rows, span), 0)
    allowed = (at <= row) & (key_ids == segcol_ref[:, 0:1]) & (back <= me)
    bias = jnp.where(allowed, 0.0, -jnp.inf).astype(jnp.float32)
    pick = (lax.broadcasted_iota(jnp.int32, (rows, rows), 1) == order_ref[:, 0:1]).astype(jnp.bfloat16)
    per_group = HQ // KVH
    trans = (((1,), (1,)), ((), ()))

    @pl.loop(0, cols)
    def _(c):
        g = (c * heads) // per_group
        kcol = pl.ds(pl.multiple_of(g * HD, HD), HD)
        vcol = pl.ds(pl.multiple_of((KVH + g) * HD, HD), HD)
        keys = jnp.concatenate([pairs_ref[:, kcol]] + [pairs_in[k, :, kcol] for k in range(REACH)], axis=0)
        values = jnp.concatenate([pairs_ref[:, vcol]] + [pairs_in[k, :, vcol] for k in range(REACH)], axis=0)
        made = []
        for h in range(heads):
            q = query_ref[:, pl.ds(pl.multiple_of(c * width + h * HD, HD), HD)]
            scores = lax.dot_general(q, keys, trans, preferred_element_type=jnp.float32)
            scores = scores * (HD ** -0.5) + bias
            top = jnp.max(scores, axis=1, keepdims=True)
            weights = jnp.exp(scores - top)
            weights = (weights / jnp.sum(weights, axis=1, keepdims=True)).astype(jnp.bfloat16)
            made.append(jnp.dot(weights, values, preferred_element_type=jnp.float32).astype(jnp.bfloat16))
        teacher = jnp.concatenate(made, axis=1)
        ordered = jnp.dot(pick, teacher, preferred_element_type=jnp.float32)
        outgoing[c] = ordered.reshape(bands, rows // bands, width).astype(jnp.bfloat16)

        @pl.loop(0, bands)
        def _(b):
            peer = b * cols + c

            @pl.when(peer != me)
            def _():
                out_copy(peer, me).start()

    own[2].start()
    for copy in own:
        copy.wait()

    @pl.loop(1, cols)
    def _(k):
        row_copy(my_band * cols + (my_col + k) % cols, k, (my_col + cols - k) % cols).wait()

    @pl.loop(1, n)
    def _(k):
        col_copy((me + k) % n, k, (me + n - k) % n).wait()
        out_copy((me + k) % n, (me + n - k) % n).wait()


def exchange(query, pairs, segment_ids, student_rows, projection, send_order):
    n = lax.axis_size("seq")
    rows = query.shape[0]
    depth = projection.shape[0]
    width = HQ * HD // COLS
    bands = n // COLS
    seg = jnp.broadcast_to(segment_ids[None, :], (8, rows))
    segcol = jnp.broadcast_to(segment_ids[:, None], (rows, HD))
    order = jnp.broadcast_to(send_order[0][:, None], (rows, HD))
    vmem = pl.BlockSpec(memory_space=pltpu.VMEM)
    hbm = pl.BlockSpec(memory_space=pl.ANY)
    dma = pltpu.SemaphoreType.DMA
    bf16 = jnp.bfloat16
    return pl.pallas_call(
        functools.partial(reach_kernel, n),
        out_shape=(
            jax.ShapeDtypeStruct((COLS, rows, student_rows.shape[1]), bf16),
            jax.ShapeDtypeStruct((n, depth, width), bf16),
            jax.ShapeDtypeStruct((n, rows // bands, width), bf16),
        ),
        in_specs=[vmem] * 5 + [hbm] * 2,
        out_specs=(hbm, hbm, hbm),
        scratch_shapes=[
            pltpu.VMEM((REACH, rows, pairs.shape[1]), bf16),
            pltpu.VMEM((REACH, 8, rows), jnp.int32),
            pltpu.VMEM((COLS, bands, rows // bands, width), bf16),
            dma((REACH,)), dma((REACH,)), dma((REACH,)), dma((REACH,)),
            dma((n,)), dma((n,)), dma((COLS,)), dma((COLS,)), dma((n,)), dma((n,)), dma((3,)),
        ],
        compiler_params=pltpu.CompilerParams(
            collective_id=0, has_side_effects=True, vmem_limit_bytes=40 * 1024 * 1024),
        name="exchange",
    )(seg, segcol, order, query, pairs, student_rows, projection)


def local(query, key, value, segment_ids, student_rows, projection, send_order):
    rows = query.shape[0]
    n = lax.axis_size("seq")
    cols = COLS
    bands = n // cols
    width = HQ * HD // cols
    depth = projection.shape[0]
    ds = student_rows.shape[1]
    share = rows // n
    near = [[b * cols + c for c in range(cols)] for b in range(bands)]

    pairs = jnp.concatenate([key, value], axis=1)
    band_rows, column, arrived = exchange(
        query, pairs, segment_ids, student_rows, projection, send_order
    )
    band_rows = band_rows.reshape(cols * rows, ds)
    column = column.reshape(n * depth, width)
    target = arrived.reshape(n, cols, share, width).transpose(1, 0, 2, 3).reshape(cols * rows, width)
    predicted = jnp.dot(band_rows, column, preferred_element_type=jnp.float32)
    residual = (predicted - target.astype(jnp.float32)).astype(jnp.bfloat16)
    proj_part = lax.dot_general(
        band_rows, residual, (((0,), (0,)), ((), ())), preferred_element_type=jnp.float32
    ).astype(jnp.bfloat16)
    proj_parts = lax.all_to_all(
        proj_part.reshape(n, depth, width), "seq", split_axis=0, concat_axis=0, tiled=True
    )
    rows_part = lax.dot_general(
        residual, column, (((1,), (1,)), ((), ())), preferred_element_type=jnp.float32
    ).astype(jnp.bfloat16)
    rows_parts = lax.all_to_all(
        rows_part.reshape(cols, rows, ds),
        "seq", split_axis=0, concat_axis=0, tiled=True, axis_index_groups=near,
    )
    grad_rows = jnp.sum(rows_parts.astype(jnp.float32), axis=0).astype(jnp.bfloat16)
    grad_scale = (rows * n) ** (-0.5)
    summed = jnp.sum(proj_parts.reshape(bands, cols, depth, width).astype(jnp.float32), axis=0)
    grad_proj = (summed * grad_scale).transpose(1, 0, 2).reshape(depth, cols * width)
    return (grad_rows, grad_proj)


def solution(mesh):
    both = ("groups", "seq")
    return jax.shard_map(
        local,
        mesh=mesh,
        in_specs=(
            P(both, None), P(both, None), P(both, None), P(both), P(both, None),
            P("seq", None), P(both, None),
        ),
        out_specs=(P(both, None), P(both, None)),
        check_vma=False,
    )
```

```python
import functools

import jax
import jax.numpy as jnp
from jax import lax
from jax.experimental import pallas as pl
from jax.experimental.pallas import tpu as pltpu
from jax.sharding import PartitionSpec as P

HQ = 32
KVH = 4
HD = 128
REACH = 3
COLS = 8
MESH = pl.DeviceIdType.MESH


def reach_kernel(n, seg_ref, segcol_ref, order_ref, query_ref, pairs_ref, rows_ref, proj_ref,
                 band_ref, column_ref, arrived_ref, pairs_in, ids_in, outgoing,
                 pair_send, pair_recv, id_send, id_recv, col_send, col_recv,
                 row_send, row_recv, out_send, out_recv, own_sem):
    me = lax.axis_index("seq")
    cols = COLS
    bands = n // cols
    my_band, my_col = me // cols, me % cols
    rows = query_ref.shape[0]
    width = HQ * HD // cols
    heads = HQ // cols

    def remote(src, dst, send, recv, peer):
        return pltpu.make_async_remote_copy(
            src_ref=src, dst_ref=dst, send_sem=send, recv_sem=recv,
            device_id={"seq": peer}, device_id_type=MESH)

    def pair_copy(k):
        return remote(pairs_ref, pairs_in.at[k - 1], pair_send.at[k - 1], pair_recv.at[k - 1], (me + k) % n)

    def id_copy(k):
        return remote(seg_ref, ids_in.at[k - 1], id_send.at[k - 1], id_recv.at[k - 1], (me + k) % n)

    def col_copy(peer, slot, place):
        block = proj_ref.at[:, pl.ds(pl.multiple_of((peer % cols) * width, width), width)]
        return remote(block, column_ref.at[place], col_send.at[slot], col_recv.at[place], peer)

    parity, chip, chips = my_col % 2, my_col // 2, cols // 2
    twin = me + 1 - 2 * parity

    def row_copy(k, place):
        peer = my_band * cols + 2 * ((chip + k) % chips) + parity
        return remote(rows_ref, band_ref.at[place], row_send.at[k], row_recv.at[place], peer)

    def twin_copy(place):
        return remote(rows_ref, band_ref.at[place], row_send.at[0], row_recv.at[place], twin)

    def pass_copy(k, source, place):
        return remote(band_ref.at[source], band_ref.at[place], row_send.at[chips + k],
                      row_recv.at[place], twin)

    def out_copy(peer, place):
        return remote(outgoing.at[peer % cols, peer // cols], arrived_ref.at[place],
                      out_send.at[peer], out_recv.at[place], peer)

    own = [
        pltpu.make_async_copy(rows_ref, band_ref.at[my_col], own_sem.at[0]),
        pltpu.make_async_copy(
            proj_ref.at[:, pl.ds(pl.multiple_of(my_col * width, width), width)],
            column_ref.at[me], own_sem.at[1]),
        pltpu.make_async_copy(outgoing.at[my_col, my_band], arrived_ref.at[me], own_sem.at[2]),
    ]

    barrier = pltpu.get_barrier_semaphore()

    @pl.loop(1, n)
    def _(k):
        pl.semaphore_signal(barrier, inc=1, device_id={"seq": (me + k) % n}, device_id_type=MESH)

    pl.semaphore_wait(barrier, n - 1)
    for k in range(1, REACH + 1):
        id_copy(k).start()
        pair_copy(k).start()
    own[0].start()
    own[1].start()

    for k in range(1, cols // 2):
        row_copy(k, my_col).start()
    twin_copy(my_col).start()

    @pl.loop(1, n)
    def _(k):
        col_copy((me + k) % n, k, me).start()

    for k in range(1, REACH + 1):
        id_copy(k).wait()
        pair_copy(k).wait()

    key_ids = jnp.concatenate([seg_ref[0:1, :]] + [ids_in[k, 0:1, :] for k in range(REACH)], axis=1)
    span = (REACH + 1) * rows
    place = lax.broadcasted_iota(jnp.int32, (rows, span), 1)
    back = place // rows
    at = place - 2 * rows * back
    row = lax.broadcasted_iota(jnp.int32, (rows, span), 0)
    allowed = (at <= row) & (key_ids == segcol_ref[:, 0:1]) & (back <= me)
    bias = jnp.where(allowed, 0.0, -jnp.inf).astype(jnp.float32)
    pick = (lax.broadcasted_iota(jnp.int32, (rows, rows), 1) == order_ref[:, 0:1]).astype(jnp.bfloat16)
    per_group = HQ // KVH
    trans = (((1,), (1,)), ((), ()))

    @pl.loop(0, cols)
    def _(c):
        g = (c * heads) // per_group
        kcol = pl.ds(pl.multiple_of(g * HD, HD), HD)
        vcol = pl.ds(pl.multiple_of((KVH + g) * HD, HD), HD)
        keys = jnp.concatenate([pairs_ref[:, kcol]] + [pairs_in[k, :, kcol] for k in range(REACH)], axis=0)
        values = jnp.concatenate([pairs_ref[:, vcol]] + [pairs_in[k, :, vcol] for k in range(REACH)], axis=0)
        made = []
        for h in range(heads):
            q = query_ref[:, pl.ds(pl.multiple_of(c * width + h * HD, HD), HD)]
            scores = lax.dot_general(q, keys, trans, preferred_element_type=jnp.float32)
            scores = scores * (HD ** -0.5) + bias
            top = jnp.max(scores, axis=1, keepdims=True)
            weights = jnp.exp(scores - top)
            weights = (weights / jnp.sum(weights, axis=1, keepdims=True)).astype(jnp.bfloat16)
            made.append(jnp.dot(weights, values, preferred_element_type=jnp.float32).astype(jnp.bfloat16))
        teacher = jnp.concatenate(made, axis=1)
        ordered = jnp.dot(pick, teacher, preferred_element_type=jnp.float32)
        outgoing[c] = ordered.reshape(bands, rows // bands, width).astype(jnp.bfloat16)

        @pl.loop(0, bands)
        def _(b):
            peer = b * cols + c

            @pl.when(peer != me)
            def _():
                out_copy(peer, me).start()

    own[2].start()
    for k in range(1, cols // 2):
        place = 2 * ((chip + chips - k) % chips) + parity
        row_copy(k, place).wait()
        pass_copy(k, place, place).start()
    for copy in own:
        copy.wait()
    twin_copy(2 * chip + 1 - parity).wait()
    for k in range(1, cols // 2):
        place = 2 * ((chip + chips - k) % chips)
        pass_copy(k, place + parity, place + 1 - parity).wait()

    @pl.loop(1, n)
    def _(k):
        col_copy((me + k) % n, k, (me + n - k) % n).wait()
        out_copy((me + k) % n, (me + n - k) % n).wait()


def exchange(query, pairs, segment_ids, student_rows, projection, send_order):
    n = lax.axis_size("seq")
    rows = query.shape[0]
    depth = projection.shape[0]
    width = HQ * HD // COLS
    bands = n // COLS
    seg = jnp.broadcast_to(segment_ids[None, :], (8, rows))
    segcol = jnp.broadcast_to(segment_ids[:, None], (rows, HD))
    order = jnp.broadcast_to(send_order[0][:, None], (rows, HD))
    vmem = pl.BlockSpec(memory_space=pltpu.VMEM)
    hbm = pl.BlockSpec(memory_space=pl.ANY)
    dma = pltpu.SemaphoreType.DMA
    bf16 = jnp.bfloat16
    return pl.pallas_call(
        functools.partial(reach_kernel, n),
        out_shape=(
            jax.ShapeDtypeStruct((COLS, rows, student_rows.shape[1]), bf16),
            jax.ShapeDtypeStruct((n, depth, width), bf16),
            jax.ShapeDtypeStruct((n, rows // bands, width), bf16),
        ),
        in_specs=[vmem] * 5 + [hbm] * 2,
        out_specs=(hbm, hbm, hbm),
        scratch_shapes=[
            pltpu.VMEM((REACH, rows, pairs.shape[1]), bf16),
            pltpu.VMEM((REACH, 8, rows), jnp.int32),
            pltpu.VMEM((COLS, bands, rows // bands, width), bf16),
            dma((REACH,)), dma((REACH,)), dma((REACH,)), dma((REACH,)),
            dma((n,)), dma((n,)), dma((COLS,)), dma((COLS,)), dma((n,)), dma((n,)), dma((3,)),
        ],
        compiler_params=pltpu.CompilerParams(
            collective_id=0, has_side_effects=True, vmem_limit_bytes=40 * 1024 * 1024),
        name="exchange",
    )(seg, segcol, order, query, pairs, student_rows, projection)


def share_kernel(n, scale, resid_ref, column_ref, part_ref, grows_ref, gproj_ref,
                 twin_out, twin_in, rows_out, rows_in, proj_in,
                 twin_send, twin_recv, row_send, row_recv, proj_send, proj_recv, own_sem):
    me = lax.axis_index("seq")
    cols = COLS
    bands = n // cols
    band, col = me // cols, me % cols
    parity, chip, chips = col % 2, col // 2, cols // 2
    twin = me + 1 - 2 * parity
    rows = grows_ref.shape[0]
    width = resid_ref.shape[1]

    def remote(src, dst, send, recv, peer):
        return pltpu.make_async_remote_copy(
            src_ref=src, dst_ref=dst, send_sem=send, recv_sem=recv,
            device_id={"seq": peer}, device_id_type=MESH)

    def proj_copy(k, place):
        peer = (me + k) % n
        return remote(part_ref.at[peer], proj_in.at[place], proj_send.at[k], proj_recv.at[place], peer)

    def twin_copy(t):
        return remote(twin_out.at[t], twin_in.at[t], twin_send.at[t], twin_recv.at[t], twin)

    def row_copy(k, place):
        t = (chip + k) % chips
        return remote(rows_out.at[k], rows_in.at[place], row_send.at[k], row_recv.at[place],
                      band * cols + 2 * t + parity)

    def product(j):
        block = resid_ref[pl.ds(pl.multiple_of(j * rows, rows), rows), :]
        return lax.dot_general(
            block, column_ref[...], (((1,), (1,)), ((), ())), preferred_element_type=jnp.float32)

    barrier = pltpu.get_barrier_semaphore()

    @pl.loop(1, n)
    def _(k):
        pl.semaphore_signal(barrier, inc=1, device_id={"seq": (me + k) % n}, device_id_type=MESH)

    pl.semaphore_wait(barrier, n - 1)

    @pl.loop(1, n)
    def _(k):
        proj_copy(k, me).start()

    own = pltpu.make_async_copy(part_ref.at[me], proj_in.at[me], own_sem.at[0])
    own.start()
    for k in range(1, cols // 2 + 1):
        t = (chip + k) % chips
        twin_out[t] = product(2 * t + 1 - parity).astype(jnp.bfloat16)
        twin_copy(t).start()
    for k in range(1, cols // 2 + 1):
        t = (chip + k) % chips
        part = product(2 * t + parity)
        twin_copy(t).wait()
        part = part + twin_in[t].astype(jnp.float32)
        if k < cols // 2:
            rows_out[k] = part.astype(jnp.bfloat16)
            row_copy(k, chip).start()
    for k in range(1, cols // 2):
        place = (chip + chips - k) % chips
        row_copy(k, place).wait()
        part = part + rows_in[place].astype(jnp.float32)
    grows_ref[...] = part.astype(jnp.bfloat16)
    own.wait()

    @pl.loop(1, n)
    def _(k):
        proj_copy(k, (me + n - k) % n).wait()

    @pl.loop(0, cols)
    def _(c):
        def add(b, total):
            return total + proj_in[b * cols + c].astype(jnp.float32)

        total = lax.fori_loop(1, bands, add, proj_in[c].astype(jnp.float32))
        gproj_ref[:, pl.ds(pl.multiple_of(c * width, width), width)] = total * scale


def share(residual, column, parts, rows, scale):
    n, depth, width = parts.shape
    ds = column.shape[0]
    vmem = pl.BlockSpec(memory_space=pltpu.VMEM)
    dma = pltpu.SemaphoreType.DMA
    bf16 = jnp.bfloat16
    half = COLS // 2
    return pl.pallas_call(
        functools.partial(share_kernel, n, scale),
        out_shape=(
            jax.ShapeDtypeStruct((rows, ds), bf16),
            jax.ShapeDtypeStruct((depth, COLS * width), jnp.float32),
        ),
        in_specs=[vmem] * 2 + [pl.BlockSpec(memory_space=pl.ANY)],
        out_specs=(vmem, vmem),
        scratch_shapes=[pltpu.VMEM((half, rows, ds), bf16)] * 4 + [
            pltpu.VMEM((n, depth, width), bf16),
            dma((half,)), dma((half,)), dma((half,)), dma((half,)), dma((n,)), dma((n,)), dma((1,)),
        ],
        compiler_params=pltpu.CompilerParams(
            collective_id=1, has_side_effects=True, vmem_limit_bytes=40 * 1024 * 1024),
        name="share",
    )(residual, column, parts)


def local(query, key, value, segment_ids, student_rows, projection, send_order):
    rows = query.shape[0]
    n = lax.axis_size("seq")
    cols = COLS
    bands = n // cols
    width = HQ * HD // cols
    depth = projection.shape[0]
    ds = student_rows.shape[1]
    each = rows // n
    pairs = jnp.concatenate([key, value], axis=1)
    band_rows, column, arrived = exchange(
        query, pairs, segment_ids, student_rows, projection, send_order
    )
    band_rows = band_rows.reshape(cols * rows, ds)
    column = column.reshape(n * depth, width)
    target = arrived.reshape(n, cols, each, width).transpose(1, 0, 2, 3).reshape(cols * rows, width)
    predicted = jnp.dot(band_rows, column, preferred_element_type=jnp.float32)
    residual = (predicted - target.astype(jnp.float32)).astype(jnp.bfloat16)
    proj_part = lax.dot_general(
        band_rows, residual, (((0,), (0,)), ((), ())), preferred_element_type=jnp.float32
    ).astype(jnp.bfloat16)
    grad_scale = (rows * n) ** (-0.5)
    grad_rows, grad_proj = share(
        residual, column, proj_part.reshape(n, depth, width), rows, grad_scale
    )
    return (grad_rows, grad_proj)


def solution(mesh):
    both = ("groups", "seq")
    return jax.shard_map(
        local,
        mesh=mesh,
        in_specs=(
            P(both, None), P(both, None), P(both, None), P(both), P(both, None),
            P("seq", None), P(both, None),
        ),
        out_specs=(P(both, None), P(both, None)),
        check_vma=False,
    )
```

```python
import functools

import jax
import jax.numpy as jnp
from jax import lax
from jax.experimental import pallas as pl
from jax.experimental.pallas import tpu as pltpu
from jax.sharding import PartitionSpec as P

HQ = 32
KVH = 4
HD = 128
REACH = 3
COLS = 8
MESH = pl.DeviceIdType.MESH


def reach_kernel(n, seg_ref, segcol_ref, order_ref, query_ref, pairs_ref, rows_ref, proj_ref,
                 band_ref, column_ref, arrived_ref, pairs_in, ids_in, outgoing,
                 pair_send, pair_recv, id_send, id_recv, col_send, col_recv,
                 row_send, row_recv, out_send, out_recv, own_sem, hop_send, hop_recv):
    me = lax.axis_index("seq")
    cols = COLS
    bands = n // cols
    my_band, my_col = me // cols, me % cols
    rows = query_ref.shape[0]
    width = HQ * HD // cols
    heads = HQ // cols

    def remote(src, dst, send, recv, peer):
        return pltpu.make_async_remote_copy(
            src_ref=src, dst_ref=dst, send_sem=send, recv_sem=recv,
            device_id={"seq": peer}, device_id_type=MESH)

    def pair_copy(k):
        return remote(pairs_ref, pairs_in.at[k - 1], pair_send.at[k - 1], pair_recv.at[k - 1], (me + k) % n)

    def id_copy(k):
        return remote(seg_ref, ids_in.at[k - 1], id_send.at[k - 1], id_recv.at[k - 1], (me + k) % n)

    def col_copy(peer, slot, place):
        block = proj_ref.at[:, pl.ds(pl.multiple_of((peer % cols) * width, width), width)]
        return remote(block, column_ref.at[place], col_send.at[slot], col_recv.at[place], peer)

    parity, chip, chips = my_col % 2, my_col // 2, cols // 2
    twin = me + 1 - 2 * parity

    def row_copy(k, place):
        peer = my_band * cols + 2 * ((chip + k) % chips) + parity
        return remote(rows_ref, band_ref.at[place], row_send.at[k], row_recv.at[place], peer)

    def twin_copy(place):
        return remote(rows_ref, band_ref.at[place], row_send.at[0], row_recv.at[place], twin)

    def pass_copy(k, source, place):
        return remote(band_ref.at[source], band_ref.at[place], row_send.at[chips + k],
                      row_recv.at[place], twin)

    def out_copy(peer, place):
        return remote(outgoing.at[peer % cols, peer // cols], arrived_ref.at[place],
                      out_send.at[peer], out_recv.at[place], peer)

    own = [
        pltpu.make_async_copy(rows_ref, band_ref.at[my_col], own_sem.at[0]),
        pltpu.make_async_copy(
            proj_ref.at[:, pl.ds(pl.multiple_of(my_col * width, width), width)],
            column_ref.at[me], own_sem.at[1]),
        pltpu.make_async_copy(outgoing.at[my_col, my_band], arrived_ref.at[me], own_sem.at[2]),
    ]

    def hop(b, way):
        slab = column_ref.at[pl.ds(b * cols, cols)]
        peer = (me + n + (cols if way == 0 else -cols)) % n
        return remote(slab, slab, hop_send.at[way, b], hop_recv.at[b], peer)

    def up(i):
        return (my_band - i >= 0) & (my_band + 1 < bands)

    def down(i):
        return (my_band + i < bands) & (my_band - 1 >= 0)

    def hops(i, first=False):
        if not first:
            @pl.when(my_band - i >= 0)
            def _():
                hop(my_band - i, 0).wait_recv()

            @pl.when(my_band + i < bands)
            def _():
                hop(my_band + i, 1).wait_recv()

        @pl.when(up(i))
        def _():
            hop(my_band - i, 0).start()

        @pl.when(down(i))
        def _():
            hop(my_band + i, 1).start()

    barrier = pltpu.get_barrier_semaphore()

    @pl.loop(1, n)
    def _(k):
        pl.semaphore_signal(barrier, inc=1, device_id={"seq": (me + k) % n}, device_id_type=MESH)

    pl.semaphore_wait(barrier, n - 1)
    own[1].start()

    @pl.loop(1, cols)
    def _(k):
        col_copy(my_band * cols + (my_col + k) % cols, k, me).start()

    for k in range(1, REACH + 1):
        id_copy(k).start()
        pair_copy(k).start()
    own[0].start()

    for k in range(1, cols // 2):
        row_copy(k, my_col).start()
    twin_copy(my_col).start()


    own[1].wait()

    @pl.loop(1, cols)
    def _(k):
        col_copy(my_band * cols + (my_col + k) % cols, k,
                 my_band * cols + (my_col + cols - k) % cols).wait()

    hops(0, True)
    for k in range(1, REACH + 1):
        id_copy(k).wait()
        pair_copy(k).wait()

    key_ids = jnp.concatenate([seg_ref[0:1, :]] + [ids_in[k, 0:1, :] for k in range(REACH)], axis=1)
    span = (REACH + 1) * rows
    place = lax.broadcasted_iota(jnp.int32, (rows, span), 1)
    back = place // rows
    at = place - 2 * rows * back
    row = lax.broadcasted_iota(jnp.int32, (rows, span), 0)
    allowed = (at <= row) & (key_ids == segcol_ref[:, 0:1]) & (back <= me)
    bias = jnp.where(allowed, 0.0, -jnp.inf).astype(jnp.float32)
    pick = (lax.broadcasted_iota(jnp.int32, (rows, rows), 1) == order_ref[:, 0:1]).astype(jnp.bfloat16)
    per_group = HQ // KVH
    trans = (((1,), (1,)), ((), ()))

    @pl.loop(0, cols)
    def _(c):
        g = (c * heads) // per_group
        kcol = pl.ds(pl.multiple_of(g * HD, HD), HD)
        vcol = pl.ds(pl.multiple_of((KVH + g) * HD, HD), HD)
        keys = jnp.concatenate([pairs_ref[:, kcol]] + [pairs_in[k, :, kcol] for k in range(REACH)], axis=0)
        values = jnp.concatenate([pairs_ref[:, vcol]] + [pairs_in[k, :, vcol] for k in range(REACH)], axis=0)
        made = []
        for h in range(heads):
            q = query_ref[:, pl.ds(pl.multiple_of(c * width + h * HD, HD), HD)]
            scores = lax.dot_general(q, keys, trans, preferred_element_type=jnp.float32)
            scores = scores * (HD ** -0.5) + bias
            top = jnp.max(scores, axis=1, keepdims=True)
            weights = jnp.exp(scores - top)
            weights = (weights / jnp.sum(weights, axis=1, keepdims=True)).astype(jnp.bfloat16)
            made.append(jnp.dot(weights, values, preferred_element_type=jnp.float32).astype(jnp.bfloat16))
        teacher = jnp.concatenate(made, axis=1)
        ordered = jnp.dot(pick, teacher, preferred_element_type=jnp.float32)
        outgoing[c] = ordered.reshape(bands, rows // bands, width).astype(jnp.bfloat16)

        @pl.loop(0, bands)
        def _(b):
            peer = b * cols + c

            @pl.when(peer != me)
            def _():
                out_copy(peer, me).start()

        @pl.when(c == cols // 2)
        def _():
            hops(1)

    own[2].start()

    @pl.loop(2, bands)
    def _(i):
        hops(i)

    for k in range(1, cols // 2):
        place = 2 * ((chip + chips - k) % chips) + parity
        row_copy(k, place).wait()
        pass_copy(k, place, place).start()
    own[0].wait()
    own[2].wait()

    @pl.loop(0, bands)
    def _(i):
        @pl.when(up(i))
        def _():
            hop(my_band - i, 0).wait_send()

        @pl.when(down(i))
        def _():
            hop(my_band + i, 1).wait_send()

    twin_copy(2 * chip + 1 - parity).wait()
    for k in range(1, cols // 2):
        place = 2 * ((chip + chips - k) % chips)
        pass_copy(k, place + parity, place + 1 - parity).wait()

    @pl.loop(1, n)
    def _(k):
        out_copy((me + k) % n, (me + n - k) % n).wait()


def exchange(query, pairs, segment_ids, student_rows, projection, send_order):
    n = lax.axis_size("seq")
    rows = query.shape[0]
    depth = projection.shape[0]
    width = HQ * HD // COLS
    bands = n // COLS
    seg = jnp.broadcast_to(segment_ids[None, :], (8, rows))
    segcol = jnp.broadcast_to(segment_ids[:, None], (rows, HD))
    order = jnp.broadcast_to(send_order[0][:, None], (rows, HD))
    vmem = pl.BlockSpec(memory_space=pltpu.VMEM)
    hbm = pl.BlockSpec(memory_space=pl.ANY)
    dma = pltpu.SemaphoreType.DMA
    bf16 = jnp.bfloat16
    return pl.pallas_call(
        functools.partial(reach_kernel, n),
        out_shape=(
            jax.ShapeDtypeStruct((COLS, rows, student_rows.shape[1]), bf16),
            jax.ShapeDtypeStruct((n, depth, width), bf16),
            jax.ShapeDtypeStruct((n, rows // bands, width), bf16),
        ),
        in_specs=[vmem] * 5 + [hbm] * 2,
        out_specs=(hbm, hbm, hbm),
        scratch_shapes=[
            pltpu.VMEM((REACH, rows, pairs.shape[1]), bf16),
            pltpu.VMEM((REACH, 8, rows), jnp.int32),
            pltpu.VMEM((COLS, bands, rows // bands, width), bf16),
            dma((REACH,)), dma((REACH,)), dma((REACH,)), dma((REACH,)),
            dma((n,)), dma((n,)), dma((COLS,)), dma((COLS,)), dma((n,)), dma((n,)), dma((3,)),
            dma((2, bands)), dma((bands,)),
        ],
        compiler_params=pltpu.CompilerParams(
            collective_id=0, has_side_effects=True, vmem_limit_bytes=40 * 1024 * 1024),
        name="exchange",
    )(seg, segcol, order, query, pairs, student_rows, projection)


def share_kernel(n, scale, resid_ref, column_ref, part_ref, grows_ref, gproj_ref,
                 twin_out, twin_in, rows_out, rows_in, proj_in,
                 twin_send, twin_recv, row_send, row_recv, proj_send, proj_recv, own_sem):
    me = lax.axis_index("seq")
    cols = COLS
    bands = n // cols
    band, col = me // cols, me % cols
    parity, chip, chips = col % 2, col // 2, cols // 2
    twin = me + 1 - 2 * parity
    rows = grows_ref.shape[0]
    width = resid_ref.shape[1]

    def remote(src, dst, send, recv, peer):
        return pltpu.make_async_remote_copy(
            src_ref=src, dst_ref=dst, send_sem=send, recv_sem=recv,
            device_id={"seq": peer}, device_id_type=MESH)

    def proj_copy(k, place):
        peer = (me + k) % n
        return remote(part_ref.at[peer], proj_in.at[place], proj_send.at[k], proj_recv.at[place], peer)

    def twin_copy(t):
        return remote(twin_out.at[t], twin_in.at[t], twin_send.at[t], twin_recv.at[t], twin)

    def row_copy(k, place):
        t = (chip + k) % chips
        return remote(rows_out.at[k], rows_in.at[place], row_send.at[k], row_recv.at[place],
                      band * cols + 2 * t + parity)

    def product(j):
        block = resid_ref[pl.ds(pl.multiple_of(j * rows, rows), rows), :]
        return lax.dot_general(
            block, column_ref[...], (((1,), (1,)), ((), ())), preferred_element_type=jnp.float32)

    barrier = pltpu.get_barrier_semaphore()

    @pl.loop(1, n)
    def _(k):
        pl.semaphore_signal(barrier, inc=1, device_id={"seq": (me + k) % n}, device_id_type=MESH)

    pl.semaphore_wait(barrier, n - 1)

    @pl.loop(1, n)
    def _(k):
        proj_copy(k, me).start()

    own = pltpu.make_async_copy(part_ref.at[me], proj_in.at[me], own_sem.at[0])
    own.start()
    for k in range(1, cols // 2 + 1):
        t = (chip + k) % chips
        twin_out[t] = product(2 * t + 1 - parity).astype(jnp.bfloat16)
        twin_copy(t).start()
    for k in range(1, cols // 2 + 1):
        t = (chip + k) % chips
        part = product(2 * t + parity)
        twin_copy(t).wait()
        part = part + twin_in[t].astype(jnp.float32)
        if k < cols // 2:
            rows_out[k] = part.astype(jnp.bfloat16)
            row_copy(k, chip).start()
    for k in range(1, cols // 2):
        place = (chip + chips - k) % chips
        row_copy(k, place).wait()
        part = part + rows_in[place].astype(jnp.float32)
    grows_ref[...] = part.astype(jnp.bfloat16)
    own.wait()

    @pl.loop(1, n)
    def _(k):
        proj_copy(k, (me + n - k) % n).wait()

    @pl.loop(0, cols)
    def _(c):
        def add(b, total):
            return total + proj_in[b * cols + c].astype(jnp.float32)

        total = lax.fori_loop(1, bands, add, proj_in[c].astype(jnp.float32))
        gproj_ref[:, pl.ds(pl.multiple_of(c * width, width), width)] = total * scale


def share(residual, column, parts, rows, scale):
    n, depth, width = parts.shape
    ds = column.shape[0]
    vmem = pl.BlockSpec(memory_space=pltpu.VMEM)
    dma = pltpu.SemaphoreType.DMA
    bf16 = jnp.bfloat16
    half = COLS // 2
    return pl.pallas_call(
        functools.partial(share_kernel, n, scale),
        out_shape=(
            jax.ShapeDtypeStruct((rows, ds), bf16),
            jax.ShapeDtypeStruct((depth, COLS * width), jnp.float32),
        ),
        in_specs=[vmem] * 2 + [pl.BlockSpec(memory_space=pl.ANY)],
        out_specs=(vmem, vmem),
        scratch_shapes=[pltpu.VMEM((half, rows, ds), bf16)] * 4 + [
            pltpu.VMEM((n, depth, width), bf16),
            dma((half,)), dma((half,)), dma((half,)), dma((half,)), dma((n,)), dma((n,)), dma((1,)),
        ],
        compiler_params=pltpu.CompilerParams(
            collective_id=1, has_side_effects=True, vmem_limit_bytes=40 * 1024 * 1024),
        name="share",
    )(residual, column, parts)


def local(query, key, value, segment_ids, student_rows, projection, send_order):
    rows = query.shape[0]
    n = lax.axis_size("seq")
    cols = COLS
    bands = n // cols
    width = HQ * HD // cols
    depth = projection.shape[0]
    ds = student_rows.shape[1]
    each = rows // n
    pairs = jnp.concatenate([key, value], axis=1)
    band_rows, column, arrived = exchange(
        query, pairs, segment_ids, student_rows, projection, send_order
    )
    band_rows = band_rows.reshape(cols * rows, ds)
    column = column.reshape(n * depth, width)
    target = arrived.reshape(n, cols, each, width).transpose(1, 0, 2, 3).reshape(cols * rows, width)
    predicted = jnp.dot(band_rows, column, preferred_element_type=jnp.float32)
    residual = (predicted - target.astype(jnp.float32)).astype(jnp.bfloat16)
    proj_part = lax.dot_general(
        band_rows, residual, (((0,), (0,)), ((), ())), preferred_element_type=jnp.float32
    ).astype(jnp.bfloat16)
    grad_scale = (rows * n) ** (-0.5)
    grad_rows, grad_proj = share(
        residual, column, proj_part.reshape(n, depth, width), rows, grad_scale
    )
    return (grad_rows, grad_proj)


def solution(mesh):
    both = ("groups", "seq")
    return jax.shard_map(
        local,
        mesh=mesh,
        in_specs=(
            P(both, None), P(both, None), P(both, None), P(both), P(both, None),
            P("seq", None), P(both, None),
        ),
        out_specs=(P(both, None), P(both, None)),
        check_vma=False,
    )
```

```python
import functools

import jax
import jax.numpy as jnp
from jax import lax
from jax.experimental import pallas as pl
from jax.experimental.pallas import tpu as pltpu
from jax.sharding import PartitionSpec as P

HQ = 32
KVH = 4
HD = 128
REACH = 3
COLS = 8
MESH = pl.DeviceIdType.MESH


def reach_kernel(n, seg_ref, segcol_ref, order_ref, query_ref, pairs_ref, rows_ref, proj_ref,
                 band_ref, column_ref, arrived_ref, pairs_in, ids_in, outgoing,
                 pair_send, pair_recv, id_send, id_recv, col_send, col_recv,
                 row_send, row_recv, out_send, out_recv, own_sem, hop_send, hop_recv):
    me = lax.axis_index("seq")
    cols = COLS
    bands = n // cols
    my_band, my_col = me // cols, me % cols
    rows = query_ref.shape[0]
    width = HQ * HD // cols
    heads = HQ // cols

    def remote(src, dst, send, recv, peer):
        return pltpu.make_async_remote_copy(
            src_ref=src, dst_ref=dst, send_sem=send, recv_sem=recv,
            device_id={"seq": peer}, device_id_type=MESH)

    def pair_copy(k):
        return remote(pairs_ref, pairs_in.at[k - 1], pair_send.at[k - 1], pair_recv.at[k - 1], (me + k) % n)

    def id_copy(k):
        return remote(seg_ref, ids_in.at[k - 1], id_send.at[k - 1], id_recv.at[k - 1], (me + k) % n)

    def col_copy(peer, slot, place):
        block = proj_ref.at[:, pl.ds(pl.multiple_of((peer % cols) * width, width), width)]
        return remote(block, column_ref.at[place], col_send.at[slot], col_recv.at[place], peer)

    parity, chip, chips = my_col % 2, my_col // 2, cols // 2
    twin = me + 1 - 2 * parity

    def row_copy(k, place):
        peer = my_band * cols + 2 * ((chip + k) % chips) + parity
        return remote(rows_ref, band_ref.at[place], row_send.at[k], row_recv.at[place], peer)

    def twin_copy(place):
        return remote(rows_ref, band_ref.at[place], row_send.at[0], row_recv.at[place], twin)

    def pass_copy(k, source, place):
        return remote(band_ref.at[source], band_ref.at[place], row_send.at[chips + k],
                      row_recv.at[place], twin)

    def out_copy(peer, place):
        return remote(outgoing.at[peer % cols, peer // cols], arrived_ref.at[place],
                      out_send.at[peer], out_recv.at[place], peer)

    own = [
        pltpu.make_async_copy(rows_ref, band_ref.at[my_col], own_sem.at[0]),
        pltpu.make_async_copy(
            proj_ref.at[:, pl.ds(pl.multiple_of(my_col * width, width), width)],
            column_ref.at[me], own_sem.at[1]),
        pltpu.make_async_copy(outgoing.at[my_col, my_band], arrived_ref.at[me], own_sem.at[2]),
    ]

    def hop(b, way):
        slab = column_ref.at[pl.ds(b * cols, cols)]
        peer = (me + n + (cols if way == 0 else -cols)) % n
        return remote(slab, slab, hop_send.at[way, b], hop_recv.at[b], peer)

    def up(i):
        return (my_band - i >= 0) & (my_band + 1 < bands)

    def down(i):
        return (my_band + i < bands) & (my_band - 1 >= 0)

    def hops(i, first=False):
        if not first:
            @pl.when(my_band - i >= 0)
            def _():
                hop(my_band - i, 0).wait_recv()

            @pl.when(my_band + i < bands)
            def _():
                hop(my_band + i, 1).wait_recv()

        @pl.when(up(i))
        def _():
            hop(my_band - i, 0).start()

        @pl.when(down(i))
        def _():
            hop(my_band + i, 1).start()

    barrier = pltpu.get_barrier_semaphore()

    @pl.loop(1, n)
    def _(k):
        pl.semaphore_signal(barrier, inc=1, device_id={"seq": (me + k) % n}, device_id_type=MESH)

    pl.semaphore_wait(barrier, n - 1)
    own[1].start()

    @pl.loop(1, cols)
    def _(k):
        col_copy(my_band * cols + (my_col + k) % cols, k, me).start()

    for k in range(1, REACH + 1):
        id_copy(k).start()
        pair_copy(k).start()
    own[0].start()

    for k in range(1, cols // 2):
        row_copy(k, my_col).start()
    twin_copy(my_col).start()


    own[1].wait()

    @pl.loop(1, cols)
    def _(k):
        col_copy(my_band * cols + (my_col + k) % cols, k,
                 my_band * cols + (my_col + cols - k) % cols).wait()

    hops(0, True)
    for k in range(1, REACH + 1):
        id_copy(k).wait()
        pair_copy(k).wait()

    key_ids = jnp.concatenate([seg_ref[0:1, :]] + [ids_in[k, 0:1, :] for k in range(REACH)], axis=1)
    span = (REACH + 1) * rows
    place = lax.broadcasted_iota(jnp.int32, (rows, span), 1)
    back = place // rows
    at = place - 2 * rows * back
    row = lax.broadcasted_iota(jnp.int32, (rows, span), 0)
    allowed = (at <= row) & (key_ids == segcol_ref[:, 0:1]) & (back <= me)
    bias = jnp.where(allowed, 0.0, -jnp.inf).astype(jnp.float32)
    pick = (lax.broadcasted_iota(jnp.int32, (rows, rows), 1) == order_ref[:, 0:1]).astype(jnp.bfloat16)
    per_group = HQ // KVH
    trans = (((1,), (1,)), ((), ()))

    @pl.loop(0, cols)
    def _(step):
        c = (step + my_col + 1) % cols
        g = (c * heads) // per_group
        kcol = pl.ds(pl.multiple_of(g * HD, HD), HD)
        vcol = pl.ds(pl.multiple_of((KVH + g) * HD, HD), HD)
        keys = jnp.concatenate([pairs_ref[:, kcol]] + [pairs_in[k, :, kcol] for k in range(REACH)], axis=0)
        values = jnp.concatenate([pairs_ref[:, vcol]] + [pairs_in[k, :, vcol] for k in range(REACH)], axis=0)
        made = []
        for h in range(heads):
            q = query_ref[:, pl.ds(pl.multiple_of(c * width + h * HD, HD), HD)]
            scores = lax.dot_general(q, keys, trans, preferred_element_type=jnp.float32)
            scores = scores * (HD ** -0.5) + bias
            top = jnp.max(scores, axis=1, keepdims=True)
            weights = jnp.exp(scores - top)
            weights = (weights * (1.0 / jnp.sum(weights, axis=1, keepdims=True))).astype(jnp.bfloat16)
            made.append(jnp.dot(weights, values, preferred_element_type=jnp.float32).astype(jnp.bfloat16))
        teacher = jnp.concatenate(made, axis=1)
        ordered = jnp.dot(pick, teacher, preferred_element_type=jnp.float32)
        outgoing[c] = ordered.reshape(bands, rows // bands, width).astype(jnp.bfloat16)

        @pl.loop(0, bands)
        def _(b):
            peer = b * cols + c

            @pl.when(peer != me)
            def _():
                out_copy(peer, me).start()

        @pl.when(step == cols // 2)
        def _():
            hops(1)

    own[2].start()

    @pl.loop(2, bands)
    def _(i):
        hops(i)

    for k in range(1, cols // 2):
        place = 2 * ((chip + chips - k) % chips) + parity
        row_copy(k, place).wait()
        pass_copy(k, place, place).start()
    own[0].wait()
    own[2].wait()

    @pl.loop(0, bands)
    def _(i):
        @pl.when(up(i))
        def _():
            hop(my_band - i, 0).wait_send()

        @pl.when(down(i))
        def _():
            hop(my_band + i, 1).wait_send()

    twin_copy(2 * chip + 1 - parity).wait()
    for k in range(1, cols // 2):
        place = 2 * ((chip + chips - k) % chips)
        pass_copy(k, place + parity, place + 1 - parity).wait()

    @pl.loop(1, n)
    def _(k):
        out_copy((me + k) % n, (me + n - k) % n).wait()


def exchange(query, pairs, segment_ids, student_rows, projection, send_order):
    n = lax.axis_size("seq")
    rows = query.shape[0]
    depth = projection.shape[0]
    width = HQ * HD // COLS
    bands = n // COLS
    seg = jnp.broadcast_to(segment_ids[None, :], (8, rows))
    segcol = jnp.broadcast_to(segment_ids[:, None], (rows, HD))
    order = jnp.broadcast_to(send_order[0][:, None], (rows, HD))
    vmem = pl.BlockSpec(memory_space=pltpu.VMEM)
    hbm = pl.BlockSpec(memory_space=pl.ANY)
    dma = pltpu.SemaphoreType.DMA
    bf16 = jnp.bfloat16
    return pl.pallas_call(
        functools.partial(reach_kernel, n),
        out_shape=(
            jax.ShapeDtypeStruct((COLS, rows, student_rows.shape[1]), bf16),
            jax.ShapeDtypeStruct((n, depth, width), bf16),
            jax.ShapeDtypeStruct((n, rows // bands, width), bf16),
        ),
        in_specs=[vmem] * 5 + [hbm] * 2,
        out_specs=(hbm, hbm, hbm),
        scratch_shapes=[
            pltpu.VMEM((REACH, rows, pairs.shape[1]), bf16),
            pltpu.VMEM((REACH, 8, rows), jnp.int32),
            pltpu.VMEM((COLS, bands, rows // bands, width), bf16),
            dma((REACH,)), dma((REACH,)), dma((REACH,)), dma((REACH,)),
            dma((n,)), dma((n,)), dma((COLS,)), dma((COLS,)), dma((n,)), dma((n,)), dma((3,)),
            dma((2, bands)), dma((bands,)),
        ],
        compiler_params=pltpu.CompilerParams(
            collective_id=0, has_side_effects=True, vmem_limit_bytes=40 * 1024 * 1024),
        name="exchange",
    )(seg, segcol, order, query, pairs, student_rows, projection)


def share_kernel(n, scale, resid_ref, column_ref, part_ref, grows_ref, gproj_ref,
                 twin_out, twin_in, rows_out, rows_in, proj_in,
                 twin_send, twin_recv, row_send, row_recv, proj_send, proj_recv, own_sem):
    me = lax.axis_index("seq")
    cols = COLS
    bands = n // cols
    band, col = me // cols, me % cols
    parity, chip, chips = col % 2, col // 2, cols // 2
    twin = me + 1 - 2 * parity
    rows = grows_ref.shape[0]
    width = resid_ref.shape[1]

    def remote(src, dst, send, recv, peer):
        return pltpu.make_async_remote_copy(
            src_ref=src, dst_ref=dst, send_sem=send, recv_sem=recv,
            device_id={"seq": peer}, device_id_type=MESH)

    def proj_copy(k, place):
        peer = (me + k) % n
        return remote(part_ref.at[peer], proj_in.at[place], proj_send.at[k], proj_recv.at[place], peer)

    def twin_copy(t):
        return remote(twin_out.at[t], twin_in.at[t], twin_send.at[t], twin_recv.at[t], twin)

    def row_copy(k, place):
        t = (chip + k) % chips
        return remote(rows_out.at[k], rows_in.at[place], row_send.at[k], row_recv.at[place],
                      band * cols + 2 * t + parity)

    def product(j):
        block = resid_ref[pl.ds(pl.multiple_of(j * rows, rows), rows), :]
        return lax.dot_general(
            block, column_ref[...], (((1,), (1,)), ((), ())), preferred_element_type=jnp.float32)

    barrier = pltpu.get_barrier_semaphore()

    @pl.loop(1, n)
    def _(k):
        pl.semaphore_signal(barrier, inc=1, device_id={"seq": (me + k) % n}, device_id_type=MESH)

    pl.semaphore_wait(barrier, n - 1)

    @pl.loop(1, n)
    def _(k):
        proj_copy(k, me).start()

    own = pltpu.make_async_copy(part_ref.at[me], proj_in.at[me], own_sem.at[0])
    own.start()
    for k in range(1, cols // 2 + 1):
        t = (chip + k) % chips
        twin_out[t] = product(2 * t + 1 - parity).astype(jnp.bfloat16)
        twin_copy(t).start()
    for k in range(1, cols // 2 + 1):
        t = (chip + k) % chips
        part = product(2 * t + parity)
        twin_copy(t).wait()
        part = part + twin_in[t].astype(jnp.float32)
        if k < cols // 2:
            rows_out[k] = part.astype(jnp.bfloat16)
            row_copy(k, chip).start()
    for k in range(1, cols // 2):
        place = (chip + chips - k) % chips
        row_copy(k, place).wait()
        part = part + rows_in[place].astype(jnp.float32)
    grows_ref[...] = part.astype(jnp.bfloat16)
    own.wait()

    @pl.loop(1, n)
    def _(k):
        proj_copy(k, (me + n - k) % n).wait()

    @pl.loop(0, cols)
    def _(c):
        def add(b, total):
            return total + proj_in[b * cols + c].astype(jnp.float32)

        total = lax.fori_loop(1, bands, add, proj_in[c].astype(jnp.float32))
        gproj_ref[:, pl.ds(pl.multiple_of(c * width, width), width)] = total * scale


def share(residual, column, parts, rows, scale):
    n, depth, width = parts.shape
    ds = column.shape[0]
    vmem = pl.BlockSpec(memory_space=pltpu.VMEM)
    dma = pltpu.SemaphoreType.DMA
    bf16 = jnp.bfloat16
    half = COLS // 2
    return pl.pallas_call(
        functools.partial(share_kernel, n, scale),
        out_shape=(
            jax.ShapeDtypeStruct((rows, ds), bf16),
            jax.ShapeDtypeStruct((depth, COLS * width), jnp.float32),
        ),
        in_specs=[vmem] * 2 + [pl.BlockSpec(memory_space=pl.ANY)],
        out_specs=(vmem, vmem),
        scratch_shapes=[pltpu.VMEM((half, rows, ds), bf16)] * 4 + [
            pltpu.VMEM((n, depth, width), bf16),
            dma((half,)), dma((half,)), dma((half,)), dma((half,)), dma((n,)), dma((n,)), dma((1,)),
        ],
        compiler_params=pltpu.CompilerParams(
            collective_id=1, has_side_effects=True, vmem_limit_bytes=40 * 1024 * 1024),
        name="share",
    )(residual, column, parts)


def local(query, key, value, segment_ids, student_rows, projection, send_order):
    rows = query.shape[0]
    n = lax.axis_size("seq")
    cols = COLS
    bands = n // cols
    width = HQ * HD // cols
    depth = projection.shape[0]
    ds = student_rows.shape[1]
    each = rows // n
    pairs = jnp.concatenate([key, value], axis=1)
    band_rows, column, arrived = exchange(
        query, pairs, segment_ids, student_rows, projection, send_order
    )
    band_rows = band_rows.reshape(cols * rows, ds)
    column = column.reshape(n * depth, width)
    place = jnp.arange(cols * rows, dtype=jnp.int32)
    owner, source, r = place // rows, (place % rows) // each, place % each
    wanted = source * (cols * each) + owner * each + r
    turn = (wanted[:, None] == place[None, :]).astype(jnp.bfloat16)
    target = jnp.dot(
        turn, arrived.reshape(cols * rows, width), preferred_element_type=jnp.float32
    )
    predicted = jnp.dot(band_rows, column, preferred_element_type=jnp.float32)
    residual = (predicted - target).astype(jnp.bfloat16)
    proj_part = lax.dot_general(
        band_rows, residual, (((0,), (0,)), ((), ())), preferred_element_type=jnp.float32
    ).astype(jnp.bfloat16)
    grad_scale = (rows * n) ** (-0.5)
    grad_rows, grad_proj = share(
        residual, column, proj_part.reshape(n, depth, width), rows, grad_scale
    )
    return (grad_rows, grad_proj)


def solution(mesh):
    both = ("groups", "seq")
    return jax.shard_map(
        local,
        mesh=mesh,
        in_specs=(
            P(both, None), P(both, None), P(both, None), P(both), P(both, None),
            P("seq", None), P(both, None),
        ),
        out_specs=(P(both, None), P(both, None)),
        check_vma=False,
    )
```

```python
import functools

import jax
import jax.numpy as jnp
from jax import lax
from jax.experimental import pallas as pl
from jax.experimental.pallas import tpu as pltpu
from jax.sharding import PartitionSpec as P

HQ = 32
KVH = 4
HD = 128
REACH = 3
COLS = 8
MESH = pl.DeviceIdType.MESH


def reach_kernel(n, seg_ref, segcol_ref, order_ref, query_ref, pairs_ref, rows_ref, proj_ref,
                 band_ref, column_ref, arrived_ref, pairs_in, ids_in, outgoing,
                 pair_send, pair_recv, id_send, id_recv, col_send, col_recv,
                 row_send, row_recv, out_send, out_recv, own_sem, hop_send, hop_recv):
    me = lax.axis_index("seq")
    cols = COLS
    bands = n // cols
    my_band, my_col = me // cols, me % cols
    rows = query_ref.shape[0]
    width = HQ * HD // cols
    heads = HQ // cols

    def remote(src, dst, send, recv, peer):
        return pltpu.make_async_remote_copy(
            src_ref=src, dst_ref=dst, send_sem=send, recv_sem=recv,
            device_id={"seq": peer}, device_id_type=MESH)

    def pair_copy(k):
        return remote(pairs_ref, pairs_in.at[k - 1], pair_send.at[k - 1], pair_recv.at[k - 1], (me + k) % n)

    def id_copy(k):
        return remote(seg_ref, ids_in.at[k - 1], id_send.at[k - 1], id_recv.at[k - 1], (me + k) % n)

    def col_copy(peer, slot, place):
        block = proj_ref.at[:, pl.ds(pl.multiple_of((peer % cols) * width, width), width)]
        return remote(block, column_ref.at[place], col_send.at[slot], col_recv.at[place], peer)

    parity, chip, chips = my_col % 2, my_col // 2, cols // 2
    twin = me + 1 - 2 * parity

    def row_copy(k, place):
        peer = my_band * cols + 2 * ((chip + k) % chips) + parity
        return remote(rows_ref, band_ref.at[place], row_send.at[k], row_recv.at[place], peer)

    def twin_copy(place):
        return remote(rows_ref, band_ref.at[place], row_send.at[0], row_recv.at[place], twin)

    def pass_copy(k, source, place):
        return remote(band_ref.at[source], band_ref.at[place], row_send.at[chips + k],
                      row_recv.at[place], twin)

    def out_copy(peer, place):
        return remote(outgoing.at[peer % cols, peer // cols], arrived_ref.at[place],
                      out_send.at[peer], out_recv.at[place], peer)

    own = [
        pltpu.make_async_copy(rows_ref, band_ref.at[my_col], own_sem.at[0]),
        pltpu.make_async_copy(
            proj_ref.at[:, pl.ds(pl.multiple_of(my_col * width, width), width)],
            column_ref.at[me], own_sem.at[1]),
        pltpu.make_async_copy(outgoing.at[my_col, my_band], arrived_ref.at[me], own_sem.at[2]),
    ]

    def hop(b, way):
        slab = column_ref.at[pl.ds(b * cols, cols)]
        peer = (me + n + (cols if way == 0 else -cols)) % n
        return remote(slab, slab, hop_send.at[way, b], hop_recv.at[b], peer)

    def up(i):
        return (my_band - i >= 0) & (my_band + 1 < bands)

    def down(i):
        return (my_band + i < bands) & (my_band - 1 >= 0)

    def hops(i, first=False):
        if not first:
            @pl.when(my_band - i >= 0)
            def _():
                hop(my_band - i, 0).wait_recv()

            @pl.when(my_band + i < bands)
            def _():
                hop(my_band + i, 1).wait_recv()

        @pl.when(up(i))
        def _():
            hop(my_band - i, 0).start()

        @pl.when(down(i))
        def _():
            hop(my_band + i, 1).start()

    barrier = pltpu.get_barrier_semaphore()

    @pl.loop(1, n)
    def _(k):
        pl.semaphore_signal(barrier, inc=1, device_id={"seq": (me + k) % n}, device_id_type=MESH)

    pl.semaphore_wait(barrier, n - 1)
    own[1].start()

    @pl.loop(1, cols)
    def _(k):
        col_copy(my_band * cols + (my_col + k) % cols, k, me).start()

    for k in range(1, REACH + 1):
        id_copy(k).start()
        pair_copy(k).start()
    own[0].start()

    for k in range(1, cols // 2):
        row_copy(k, my_col).start()
    twin_copy(my_col).start()


    own[1].wait()

    @pl.loop(1, cols)
    def _(k):
        col_copy(my_band * cols + (my_col + k) % cols, k,
                 my_band * cols + (my_col + cols - k) % cols).wait()

    hops(0, True)
    for k in range(1, REACH + 1):
        id_copy(k).wait()
        pair_copy(k).wait()

    key_ids = jnp.concatenate([seg_ref[0:1, :]] + [ids_in[k, 0:1, :] for k in range(REACH)], axis=1)
    span = (REACH + 1) * rows
    place = lax.broadcasted_iota(jnp.int32, (rows, span), 1)
    back = place // rows
    at = place - 2 * rows * back
    row = lax.broadcasted_iota(jnp.int32, (rows, span), 0)
    allowed = (at <= row) & (key_ids == segcol_ref[:, 0:1]) & (back <= me)
    bias = jnp.where(allowed, 0.0, -jnp.inf).astype(jnp.float32)
    pick = (lax.broadcasted_iota(jnp.int32, (rows, rows), 1) == order_ref[:, 0:1]).astype(jnp.bfloat16)
    per_group = HQ // KVH
    trans = (((1,), (1,)), ((), ()))

    @pl.loop(0, cols)
    def _(step):
        c = (step + my_col + 1) % cols
        g = (c * heads) // per_group
        kcol = pl.ds(pl.multiple_of(g * HD, HD), HD)
        vcol = pl.ds(pl.multiple_of((KVH + g) * HD, HD), HD)
        keys = jnp.concatenate([pairs_ref[:, kcol]] + [pairs_in[k, :, kcol] for k in range(REACH)], axis=0)
        values = jnp.concatenate([pairs_ref[:, vcol]] + [pairs_in[k, :, vcol] for k in range(REACH)], axis=0)
        made = []
        for h in range(heads):
            q = query_ref[:, pl.ds(pl.multiple_of(c * width + h * HD, HD), HD)]
            scores = lax.dot_general(q, keys, trans, preferred_element_type=jnp.float32)
            scores = scores * (HD ** -0.5) + bias
            top = jnp.max(scores, axis=1, keepdims=True)
            weights = jnp.exp(scores - top)
            weights = (weights * (1.0 / jnp.sum(weights, axis=1, keepdims=True))).astype(jnp.bfloat16)
            made.append(jnp.dot(weights, values, preferred_element_type=jnp.float32).astype(jnp.bfloat16))
        teacher = jnp.concatenate(made, axis=1)
        ordered = jnp.dot(pick, teacher, preferred_element_type=jnp.float32)
        outgoing[c] = ordered.reshape(bands, rows // bands, width).astype(jnp.bfloat16)

        @pl.loop(0, bands)
        def _(b):
            peer = ((my_band + 1 + b) % bands) * cols + c

            @pl.when(peer != me)
            def _():
                out_copy(peer, me).start()

        @pl.when(step == 1)
        def _():
            hops(1)

        @pl.when(step == cols // 2)
        def _():
            for k in range(1, cols // 2):
                place = 2 * ((chip + chips - k) % chips) + parity
                row_copy(k, place).wait()
                pass_copy(k, place, place).start()

    own[2].start()

    @pl.loop(2, bands)
    def _(i):
        hops(i)

    own[0].wait()
    own[2].wait()

    @pl.loop(0, bands)
    def _(i):
        @pl.when(up(i))
        def _():
            hop(my_band - i, 0).wait_send()

        @pl.when(down(i))
        def _():
            hop(my_band + i, 1).wait_send()

    twin_copy(2 * chip + 1 - parity).wait()
    for k in range(1, cols // 2):
        place = 2 * ((chip + chips - k) % chips)
        pass_copy(k, place + parity, place + 1 - parity).wait()

    @pl.loop(1, n)
    def _(k):
        out_copy((me + k) % n, (me + n - k) % n).wait()


def exchange(query, pairs, segment_ids, student_rows, projection, send_order):
    n = lax.axis_size("seq")
    rows = query.shape[0]
    depth = projection.shape[0]
    width = HQ * HD // COLS
    bands = n // COLS
    seg = jnp.broadcast_to(segment_ids[None, :], (8, rows))
    segcol = jnp.broadcast_to(segment_ids[:, None], (rows, HD))
    order = jnp.broadcast_to(send_order[0][:, None], (rows, HD))
    vmem = pl.BlockSpec(memory_space=pltpu.VMEM)
    dma = pltpu.SemaphoreType.DMA
    bf16 = jnp.bfloat16
    return pl.pallas_call(
        functools.partial(reach_kernel, n),
        out_shape=(
            jax.ShapeDtypeStruct((COLS, rows, student_rows.shape[1]), bf16),
            jax.ShapeDtypeStruct((n, depth, width), bf16),
            jax.ShapeDtypeStruct((n, rows // bands, width), bf16),
        ),
        in_specs=[vmem] * 7,
        out_specs=(vmem, vmem, vmem),
        scratch_shapes=[
            pltpu.VMEM((REACH, rows, pairs.shape[1]), bf16),
            pltpu.VMEM((REACH, 8, rows), jnp.int32),
            pltpu.VMEM((COLS, bands, rows // bands, width), bf16),
            dma((REACH,)), dma((REACH,)), dma((REACH,)), dma((REACH,)),
            dma((n,)), dma((n,)), dma((COLS,)), dma((COLS,)), dma((n,)), dma((n,)), dma((3,)),
            dma((2, bands)), dma((bands,)),
        ],
        compiler_params=pltpu.CompilerParams(
            collective_id=0, has_side_effects=True, vmem_limit_bytes=40 * 1024 * 1024),
        name="exchange",
    )(seg, segcol, order, query, pairs, student_rows, projection)


def share_kernel(n, scale, resid_ref, column_ref, part_ref, grows_ref, gproj_ref,
                 twin_out, twin_in, rows_out, rows_in, sum_in, sum_out, fin_in, fin_out,
                 twin_send, twin_recv, row_send, row_recv, sum_send, sum_recv, fin_send, fin_recv):
    me = lax.axis_index("seq")
    cols = COLS
    bands = n // cols
    band, col = me // cols, me % cols
    parity, chip, chips = col % 2, col // 2, cols // 2
    twin = me + 1 - 2 * parity
    rows = grows_ref.shape[0]
    width = resid_ref.shape[1]

    def remote(src, dst, send, recv, peer):
        return pltpu.make_async_remote_copy(
            src_ref=src, dst_ref=dst, send_sem=send, recv_sem=recv,
            device_id={"seq": peer}, device_id_type=MESH)

    def sum_copy(way, t):
        peer = (me + n + (cols if way == 0 else -cols)) % n
        return remote(sum_out.at[way, t], sum_in.at[way, t],
                      sum_send.at[way, t], sum_recv.at[way, t], peer)

    def fin_copy(k, place):
        j = (col + k) % cols
        return remote(fin_out.at[j], fin_in.at[place], fin_send.at[k], fin_recv.at[place],
                      band * cols + j)

    def slab(b):
        return part_ref[pl.ds(b * cols, cols)].astype(jnp.float32)

    def chain(step):
        for way, t, more, start in (
            (0, bands - 1 - step, bands - 1 - step > band, band == 0),
            (1, step, step < band, band == bands - 1),
        ):
            @pl.when(more & start)
            def _():
                sum_out[way, t] = slab(t).astype(sum_out.dtype)

            @pl.when(more & jnp.logical_not(start))
            def _():
                sum_copy(way, t).wait_recv()
                total = slab(t) + sum_in[way, t].astype(jnp.float32)
                sum_out[way, t] = total.astype(sum_out.dtype)

            @pl.when(more)
            def _():
                sum_copy(way, t).start()

    def twin_copy(t):
        return remote(twin_out.at[t], twin_in.at[t], twin_send.at[t], twin_recv.at[t], twin)

    def row_copy(k, place):
        t = (chip + k) % chips
        return remote(rows_out.at[k], rows_in.at[place], row_send.at[k], row_recv.at[place],
                      band * cols + 2 * t + parity)

    def product(j):
        block = resid_ref[pl.ds(pl.multiple_of(j * rows, rows), rows), :]
        return lax.dot_general(
            block, column_ref[...], (((1,), (1,)), ((), ())), preferred_element_type=jnp.float32)

    barrier = pltpu.get_barrier_semaphore()

    @pl.loop(1, n)
    def _(k):
        pl.semaphore_signal(barrier, inc=1, device_id={"seq": (me + k) % n}, device_id_type=MESH)

    pl.semaphore_wait(barrier, n - 1)

    for k in range(1, cols // 2 + 1):
        t = (chip + k) % chips
        twin_out[t] = product(2 * t + 1 - parity).astype(jnp.bfloat16)
        twin_copy(t).start()
    chain(0)
    for k in range(1, cols // 2 + 1):
        t = (chip + k) % chips
        part = product(2 * t + parity)
        twin_copy(t).wait()
        part = part + twin_in[t].astype(jnp.float32)
        if k < cols // 2:
            rows_out[k] = part.astype(jnp.bfloat16)
            row_copy(k, chip).start()
    @pl.loop(1, bands - 1)
    def _(step):
        chain(step)

    for way, there in ((0, band > 0), (1, band < bands - 1)):
        @pl.when(there)
        def _():
            sum_copy(way, band).wait_recv()

    @pl.when((band > 0) & (band < bands - 1))
    def _():
        fin_out[...] = (slab(band) + sum_in[0, band].astype(jnp.float32)
                        + sum_in[1, band].astype(jnp.float32)).astype(jnp.bfloat16)

    @pl.when(band == 0)
    def _():
        fin_out[...] = (slab(band) + sum_in[1, band].astype(jnp.float32)).astype(jnp.bfloat16)

    @pl.when((band > 0) & (band == bands - 1))
    def _():
        fin_out[...] = (slab(band) + sum_in[0, band].astype(jnp.float32)).astype(jnp.bfloat16)

    fin_in[col] = fin_out[col]
    for k in range(1, cols):
        fin_copy(k, col).start()
    for k in range(1, cols // 2):
        place = (chip + chips - k) % chips
        row_copy(k, place).wait()
        part = part + rows_in[place].astype(jnp.float32)
    grows_ref[...] = part.astype(jnp.bfloat16)
    for k in range(1, cols):
        fin_copy(k, (col + cols - k) % cols).wait()
    for c in range(cols):
        gproj_ref[:, c * width : (c + 1) * width] = fin_in[c].astype(jnp.float32) * scale

    @pl.loop(0, bands)
    def _(t):
        @pl.when((t > band))
        def _():
            sum_copy(0, t).wait_send()

        @pl.when((t < band))
        def _():
            sum_copy(1, t).wait_send()


def share(residual, column, parts, rows, scale):
    n, depth, width = parts.shape
    ds = column.shape[0]
    vmem = pl.BlockSpec(memory_space=pltpu.VMEM)
    dma = pltpu.SemaphoreType.DMA
    bf16 = jnp.bfloat16
    half = COLS // 2
    wire = bf16 if n // COLS <= 4 else jnp.float32
    return pl.pallas_call(
        functools.partial(share_kernel, n, scale),
        out_shape=(
            jax.ShapeDtypeStruct((rows, ds), bf16),
            jax.ShapeDtypeStruct((depth, COLS * width), jnp.float32),
        ),
        in_specs=[vmem] * 3,
        out_specs=(vmem, vmem),
        scratch_shapes=[pltpu.VMEM((half, rows, ds), bf16)] * 4 + [
            pltpu.VMEM((2, n // COLS, COLS, depth, width), wire),
            pltpu.VMEM((2, n // COLS, COLS, depth, width), wire),
            pltpu.VMEM((COLS, depth, width), bf16),
            pltpu.VMEM((COLS, depth, width), bf16),
            dma((half,)), dma((half,)), dma((half,)), dma((half,)),
            dma((2, n // COLS)), dma((2, n // COLS)), dma((COLS,)), dma((COLS,)),
        ],
        compiler_params=pltpu.CompilerParams(
            collective_id=1, has_side_effects=True, vmem_limit_bytes=40 * 1024 * 1024),
        name="share",
    )(residual, column, parts)


def local(query, key, value, segment_ids, student_rows, projection, send_order):
    rows = query.shape[0]
    n = lax.axis_size("seq")
    cols = COLS
    bands = n // cols
    width = HQ * HD // cols
    depth = projection.shape[0]
    ds = student_rows.shape[1]
    each = rows // n
    pairs = jnp.concatenate([key, value], axis=1)
    band_rows, column, arrived = exchange(
        query, pairs, segment_ids, student_rows, projection, send_order
    )
    band_rows = band_rows.reshape(cols * rows, ds)
    column = column.reshape(n * depth, width)
    place = jnp.arange(cols * rows, dtype=jnp.int32)
    owner, source, r = place // rows, (place % rows) // each, place % each
    wanted = source * (cols * each) + owner * each + r
    turn = (wanted[:, None] == place[None, :]).astype(jnp.bfloat16)
    target = jnp.dot(
        turn, arrived.reshape(cols * rows, width), preferred_element_type=jnp.float32
    )
    predicted = jnp.dot(band_rows, column, preferred_element_type=jnp.float32)
    residual = (predicted - target).astype(jnp.bfloat16)
    proj_part = lax.dot_general(
        band_rows, residual, (((0,), (0,)), ((), ())), preferred_element_type=jnp.float32
    ).astype(jnp.bfloat16)
    grad_scale = (rows * n) ** (-0.5)
    grad_rows, grad_proj = share(
        residual, column, proj_part.reshape(n, depth, width), rows, grad_scale
    )
    return (grad_rows, grad_proj)


def solution(mesh):
    both = ("groups", "seq")
    return jax.shard_map(
        local,
        mesh=mesh,
        in_specs=(
            P(both, None), P(both, None), P(both, None), P(both), P(both, None),
            P("seq", None), P(both, None),
        ),
        out_specs=(P(both, None), P(both, None)),
        check_vma=False,
    )
```

```python
import functools

import jax
import jax.numpy as jnp
from jax import lax
from jax.experimental import pallas as pl
from jax.experimental.pallas import tpu as pltpu
from jax.sharding import PartitionSpec as P

HQ = 32
KVH = 4
HD = 128
REACH = 3
COLS = 8
MESH = pl.DeviceIdType.MESH


def reach_kernel(n, seg_ref, segcol_ref, order_ref, query_ref, pairs_ref, rows_ref, proj_ref,
                 band_ref, column_ref, arrived_ref, pairs_in, ids_in, outgoing,
                 pair_send, pair_recv, id_send, id_recv, col_send, col_recv,
                 row_send, row_recv, out_send, out_recv, own_sem, hop_send, hop_recv):
    me = lax.axis_index("seq")
    cols = COLS
    bands = n // cols
    my_band, my_col = me // cols, me % cols
    rows = query_ref.shape[0]
    width = HQ * HD // cols
    heads = HQ // cols

    def remote(src, dst, send, recv, peer):
        return pltpu.make_async_remote_copy(
            src_ref=src, dst_ref=dst, send_sem=send, recv_sem=recv,
            device_id={"seq": peer}, device_id_type=MESH)

    def pair_copy(k):
        return remote(pairs_ref, pairs_in.at[k - 1], pair_send.at[k - 1], pair_recv.at[k - 1], (me + k) % n)

    def id_copy(k):
        return remote(seg_ref, ids_in.at[k - 1], id_send.at[k - 1], id_recv.at[k - 1], (me + k) % n)

    def col_copy(peer, slot, place):
        block = proj_ref.at[:, pl.ds(pl.multiple_of((peer % cols) * width, width), width)]
        return remote(block, column_ref.at[place], col_send.at[slot], col_recv.at[place], peer)

    parity, chip, chips = my_col % 2, my_col // 2, cols // 2
    twin = me + 1 - 2 * parity

    def row_copy(k, place):
        peer = my_band * cols + 2 * ((chip + k) % chips) + parity
        return remote(rows_ref, band_ref.at[place], row_send.at[k], row_recv.at[place], peer)

    def twin_copy(place):
        return remote(rows_ref, band_ref.at[place], row_send.at[0], row_recv.at[place], twin)

    def pass_copy(k, source, place):
        return remote(band_ref.at[source], band_ref.at[place], row_send.at[chips + k],
                      row_recv.at[place], twin)

    def out_copy(peer, place):
        return remote(outgoing.at[peer % cols, peer // cols], arrived_ref.at[place],
                      out_send.at[peer], out_recv.at[place], peer)

    own = [
        pltpu.make_async_copy(rows_ref, band_ref.at[my_col], own_sem.at[0]),
        pltpu.make_async_copy(
            proj_ref.at[:, pl.ds(pl.multiple_of(my_col * width, width), width)],
            column_ref.at[me], own_sem.at[1]),
        pltpu.make_async_copy(outgoing.at[my_col, my_band], arrived_ref.at[me], own_sem.at[2]),
    ]

    def hop(b, way):
        slab = column_ref.at[pl.ds(b * cols, cols)]
        peer = (me + n + (cols if way == 0 else -cols)) % n
        return remote(slab, slab, hop_send.at[way, b], hop_recv.at[b], peer)

    def up(i):
        return (my_band - i >= 0) & (my_band + 1 < bands)

    def down(i):
        return (my_band + i < bands) & (my_band - 1 >= 0)

    def hops(i, first=False):
        if not first:
            @pl.when(my_band - i >= 0)
            def _():
                hop(my_band - i, 0).wait_recv()

            @pl.when(my_band + i < bands)
            def _():
                hop(my_band + i, 1).wait_recv()

        @pl.when(up(i))
        def _():
            hop(my_band - i, 0).start()

        @pl.when(down(i))
        def _():
            hop(my_band + i, 1).start()

    barrier = pltpu.get_barrier_semaphore()

    @pl.loop(1, n)
    def _(k):
        pl.semaphore_signal(barrier, inc=1, device_id={"seq": (me + k) % n}, device_id_type=MESH)

    pl.semaphore_wait(barrier, n - 1)
    own[1].start()

    @pl.loop(1, cols)
    def _(k):
        col_copy(my_band * cols + (my_col + k) % cols, k, me).start()

    for k in range(1, REACH + 1):
        id_copy(k).start()
        pair_copy(k).start()
    own[0].start()

    for k in range(1, cols // 2):
        row_copy(k, my_col).start()
    twin_copy(my_col).start()


    own[1].wait()

    @pl.loop(1, cols)
    def _(k):
        col_copy(my_band * cols + (my_col + k) % cols, k,
                 my_band * cols + (my_col + cols - k) % cols).wait()

    hops(0, True)
    for k in range(1, REACH + 1):
        id_copy(k).wait()
        pair_copy(k).wait()

    key_ids = jnp.concatenate([seg_ref[0:1, :]] + [ids_in[k, 0:1, :] for k in range(REACH)], axis=1)
    span = (REACH + 1) * rows
    place = lax.broadcasted_iota(jnp.int32, (rows, span), 1)
    back = place // rows
    at = place - 2 * rows * back
    row = lax.broadcasted_iota(jnp.int32, (rows, span), 0)
    allowed = (at <= row) & (key_ids == segcol_ref[:, 0:1]) & (back <= me)
    bias = jnp.where(allowed, 0.0, -jnp.inf).astype(jnp.float32)
    pick = (lax.broadcasted_iota(jnp.int32, (rows, rows), 1) == order_ref[:, 0:1]).astype(jnp.bfloat16)
    per_group = HQ // KVH
    trans = (((1,), (1,)), ((), ()))

    @pl.loop(0, cols)
    def _(step):
        c = (step + my_col + 1) % cols
        g = (c * heads) // per_group
        kcol = pl.ds(pl.multiple_of(g * HD, HD), HD)
        vcol = pl.ds(pl.multiple_of((KVH + g) * HD, HD), HD)
        keys = jnp.concatenate([pairs_ref[:, kcol]] + [pairs_in[k, :, kcol] for k in range(REACH)], axis=0)
        values = jnp.concatenate([pairs_ref[:, vcol]] + [pairs_in[k, :, vcol] for k in range(REACH)], axis=0)
        made = []
        for h in range(heads):
            q = query_ref[:, pl.ds(pl.multiple_of(c * width + h * HD, HD), HD)]
            scores = lax.dot_general(q, keys, trans, preferred_element_type=jnp.float32)
            scores = scores * (HD ** -0.5) + bias
            top = jnp.max(scores, axis=1, keepdims=True)
            weights = jnp.exp(scores - top)
            weights = (weights * (1.0 / jnp.sum(weights, axis=1, keepdims=True))).astype(jnp.bfloat16)
            made.append(jnp.dot(weights, values, preferred_element_type=jnp.float32).astype(jnp.bfloat16))
        teacher = jnp.concatenate(made, axis=1)
        ordered = jnp.dot(pick, teacher, preferred_element_type=jnp.float32)
        outgoing[c] = ordered.reshape(bands, rows // bands, width).astype(jnp.bfloat16)

        @pl.loop(0, bands)
        def _(b):
            peer = ((my_band + 1 + b) % bands) * cols + c

            @pl.when(peer != me)
            def _():
                out_copy(peer, me).start()

        @pl.when(step == 1)
        def _():
            hops(1)

        @pl.when(step == cols // 2)
        def _():
            for k in range(1, cols // 2):
                place = 2 * ((chip + chips - k) % chips) + parity
                row_copy(k, place).wait()
                pass_copy(k, place, place).start()

    own[2].start()

    @pl.loop(2, bands)
    def _(i):
        hops(i)

    own[0].wait()
    own[2].wait()

    @pl.loop(0, bands)
    def _(i):
        @pl.when(up(i))
        def _():
            hop(my_band - i, 0).wait_send()

        @pl.when(down(i))
        def _():
            hop(my_band + i, 1).wait_send()

    twin_copy(2 * chip + 1 - parity).wait()
    for k in range(1, cols // 2):
        place = 2 * ((chip + chips - k) % chips)
        pass_copy(k, place + parity, place + 1 - parity).wait()

    @pl.loop(1, n)
    def _(k):
        out_copy((me + k) % n, (me + n - k) % n).wait()


def exchange(query, pairs, segment_ids, student_rows, projection, send_order):
    n = lax.axis_size("seq")
    rows = query.shape[0]
    depth = projection.shape[0]
    width = HQ * HD // COLS
    bands = n // COLS
    seg = jnp.broadcast_to(segment_ids[None, :], (8, rows))
    segcol = jnp.broadcast_to(segment_ids[:, None], (rows, HD))
    order = jnp.broadcast_to(send_order[0][:, None], (rows, HD))
    vmem = pl.BlockSpec(memory_space=pltpu.VMEM)
    dma = pltpu.SemaphoreType.DMA
    bf16 = jnp.bfloat16
    return pl.pallas_call(
        functools.partial(reach_kernel, n),
        out_shape=(
            jax.ShapeDtypeStruct((COLS, rows, student_rows.shape[1]), bf16),
            jax.ShapeDtypeStruct((n, depth, width), bf16),
            jax.ShapeDtypeStruct((n, rows // bands, width), bf16),
        ),
        in_specs=[vmem] * 7,
        out_specs=(vmem, vmem, vmem),
        scratch_shapes=[
            pltpu.VMEM((REACH, rows, pairs.shape[1]), bf16),
            pltpu.VMEM((REACH, 8, rows), jnp.int32),
            pltpu.VMEM((COLS, bands, rows // bands, width), bf16),
            dma((REACH,)), dma((REACH,)), dma((REACH,)), dma((REACH,)),
            dma((n,)), dma((n,)), dma((COLS,)), dma((COLS,)), dma((n,)), dma((n,)), dma((3,)),
            dma((2, bands)), dma((bands,)),
        ],
        compiler_params=pltpu.CompilerParams(
            collective_id=0, has_side_effects=True, vmem_limit_bytes=40 * 1024 * 1024),
        name="exchange",
    )(seg, segcol, order, query, pairs, student_rows, projection)


def share_kernel(n, scale, resid_ref, column_ref, part_ref, grows_ref, gproj_ref,
                 twin_out, twin_in, rows_out, rows_in, proj_in,
                 twin_send, twin_recv, row_send, row_recv, proj_send, proj_recv, own_sem):
    me = lax.axis_index("seq")
    cols = COLS
    bands = n // cols
    band, col = me // cols, me % cols
    parity, chip, chips = col % 2, col // 2, cols // 2
    twin = me + 1 - 2 * parity
    rows = grows_ref.shape[0]
    width = resid_ref.shape[1]

    def remote(src, dst, send, recv, peer):
        return pltpu.make_async_remote_copy(
            src_ref=src, dst_ref=dst, send_sem=send, recv_sem=recv,
            device_id={"seq": peer}, device_id_type=MESH)

    def proj_copy(k, place):
        peer = (me + k) % n
        return remote(part_ref.at[peer], proj_in.at[place], proj_send.at[k], proj_recv.at[place], peer)

    def twin_copy(t):
        return remote(twin_out.at[t], twin_in.at[t], twin_send.at[t], twin_recv.at[t], twin)

    def row_copy(k, place):
        t = (chip + k) % chips
        return remote(rows_out.at[k], rows_in.at[place], row_send.at[k], row_recv.at[place],
                      band * cols + 2 * t + parity)

    def product(j):
        block = resid_ref[pl.ds(pl.multiple_of(j * rows, rows), rows), :]
        return lax.dot_general(
            block, column_ref[...], (((1,), (1,)), ((), ())), preferred_element_type=jnp.float32)

    barrier = pltpu.get_barrier_semaphore()

    @pl.loop(1, n)
    def _(k):
        pl.semaphore_signal(barrier, inc=1, device_id={"seq": (me + k) % n}, device_id_type=MESH)

    pl.semaphore_wait(barrier, n - 1)

    @pl.loop(1, n)
    def _(k):
        proj_copy(k, me).start()

    own = pltpu.make_async_copy(part_ref.at[me], proj_in.at[me], own_sem.at[0])
    own.start()
    for k in range(1, cols // 2 + 1):
        t = (chip + k) % chips
        twin_out[t] = product(2 * t + 1 - parity).astype(jnp.bfloat16)
        twin_copy(t).start()
    for k in range(1, cols // 2 + 1):
        t = (chip + k) % chips
        part = product(2 * t + parity)
        twin_copy(t).wait()
        part = part + twin_in[t].astype(jnp.float32)
        if k < cols // 2:
            rows_out[k] = part.astype(jnp.bfloat16)
            row_copy(k, chip).start()
    for k in range(1, cols // 2):
        place = (chip + chips - k) % chips
        row_copy(k, place).wait()
        part = part + rows_in[place].astype(jnp.float32)
    grows_ref[...] = part.astype(jnp.bfloat16)
    own.wait()

    @pl.loop(1, n)
    def _(k):
        proj_copy(k, (me + n - k) % n).wait()

    @pl.loop(0, cols)
    def _(c):
        def add(b, total):
            return total + proj_in[b * cols + c].astype(jnp.float32)

        total = lax.fori_loop(1, bands, add, proj_in[c].astype(jnp.float32))
        gproj_ref[:, pl.ds(pl.multiple_of(c * width, width), width)] = total * scale


def share(residual, column, parts, rows, scale):
    n, depth, width = parts.shape
    ds = column.shape[0]
    vmem = pl.BlockSpec(memory_space=pltpu.VMEM)
    dma = pltpu.SemaphoreType.DMA
    bf16 = jnp.bfloat16
    half = COLS // 2
    return pl.pallas_call(
        functools.partial(share_kernel, n, scale),
        out_shape=(
            jax.ShapeDtypeStruct((rows, ds), bf16),
            jax.ShapeDtypeStruct((depth, COLS * width), jnp.float32),
        ),
        in_specs=[vmem] * 3,
        out_specs=(vmem, vmem),
        scratch_shapes=[pltpu.VMEM((half, rows, ds), bf16)] * 4 + [
            pltpu.VMEM((n, depth, width), bf16),
            dma((half,)), dma((half,)), dma((half,)), dma((half,)), dma((n,)), dma((n,)), dma((1,)),
        ],
        compiler_params=pltpu.CompilerParams(
            collective_id=1, has_side_effects=True, vmem_limit_bytes=40 * 1024 * 1024),
        name="share",
    )(residual, column, parts)


def local(query, key, value, segment_ids, student_rows, projection, send_order):
    rows = query.shape[0]
    n = lax.axis_size("seq")
    cols = COLS
    bands = n // cols
    width = HQ * HD // cols
    depth = projection.shape[0]
    ds = student_rows.shape[1]
    each = rows // n
    pairs = jnp.concatenate([key, value], axis=1)
    band_rows, column, arrived = exchange(
        query, pairs, segment_ids, student_rows, projection, send_order
    )
    band_rows = band_rows.reshape(cols * rows, ds)
    column = column.reshape(n * depth, width)
    place = jnp.arange(cols * rows, dtype=jnp.int32)
    owner, source, r = place // rows, (place % rows) // each, place % each
    wanted = source * (cols * each) + owner * each + r
    turn = (wanted[:, None] == place[None, :]).astype(jnp.bfloat16)
    target = jnp.dot(
        turn, arrived.reshape(cols * rows, width), preferred_element_type=jnp.float32
    )
    predicted = jnp.dot(band_rows, column, preferred_element_type=jnp.float32)
    residual = (predicted - target).astype(jnp.bfloat16)
    proj_part = lax.dot_general(
        band_rows, residual, (((0,), (0,)), ((), ())), preferred_element_type=jnp.float32
    ).astype(jnp.bfloat16)
    grad_scale = (rows * n) ** (-0.5)
    grad_rows, grad_proj = share(
        residual, column, proj_part.reshape(n, depth, width), rows, grad_scale
    )
    return (grad_rows, grad_proj)


def solution(mesh):
    both = ("groups", "seq")
    return jax.shard_map(
        local,
        mesh=mesh,
        in_specs=(
            P(both, None), P(both, None), P(both, None), P(both), P(both, None),
            P("seq", None), P(both, None),
        ),
        out_specs=(P(both, None), P(both, None)),
        check_vma=False,
    )
```
